256 devices in a mesh: seq: 128 (over x, z_hi, y, core), head: 2 (over z_lo).
Axes of the slice: x: 4, y: 4, z: 8 (z_hi: 4, z_lo: 2; z = z_hi * 2 + z_lo), core: 2. Of those that a mesh axis runs over, the one named last changes fastest.
Arguments:
- cur_query: bfloat16 [16384, 1536], P('seq', 'head'), may hold values from -6 to 6
- cur_key: bfloat16 [16384, 1536], P('seq', 'head'), may hold values from -6 to 6
- cur_value: bfloat16 [16384, 1536], P('seq', 'head'), may hold values from -6 to 6
- grad_out: bfloat16 [16384, 1536], P('seq', 'head'), may hold values from -6 to 6
- out_weight: bfloat16 [1536, 1536], P(None, 'head'), may hold values from -0.15625 to 0.15625
- half_key: bfloat16 [3840, 1536], P('seq', 'head'), may hold values from -6 to 6
- half_value: bfloat16 [3840, 1536], P('seq', 'head'), may hold values from -6 to 6
- quart_key: bfloat16 [1024, 1536], P('seq', 'head'), may hold values from -6 to 6
- quart_value: bfloat16 [1024, 1536], P('seq', 'head'), may hold values from -6 to 6
- cur_count: int32 [16, 8], replicated, may hold values from 1 to 128, 960 in all within a row
- section_bias: float32 [2, 24], P(None, 'head'), may hold values from -1 to 1
Outputs:
- d_query: bfloat16 [16384, 1536], P('seq', 'head')
- d_key: bfloat16 [16384, 1536], P('seq', 'head')
- d_value: bfloat16 [16384, 1536], P('seq', 'head')
- d_half_key: bfloat16 [3840, 1536], P('seq', 'head')
- d_half_value: bfloat16 [3840, 1536], P('seq', 'head')
- d_quart_key: bfloat16 [1024, 1536], P('seq', 'head')
- d_quart_value: bfloat16 [1024, 1536], P('seq', 'head')
- d_section_bias: float32 [2, 24], P(None, 'head')
The draws below stay inside these ranges and needn't reach their ends.
Inputs may be any that keep to these rules, and one draw needn't show every extreme that they name: The first cur_count[c, s] slots of shard s of clip c hold real tokens, the rest padding; every row sums to 960 and its largest entry is 128.
All inputs are finite; a program needn't handle non-finite values.
Results may differ from the reference program's by a relative error of at most 0.025.
Values may be sent and summed in bfloat16 or wider, within the bound.
A program may use at most 128 MiB of HBM per device.

```python
import math
import jax
import jax.numpy as jnp
import numpy as np
from jax import lax

D = 1536
HEADS = 24
HD = 64
GROUP = 8
C_DEV = 128
FRAME_TOK = 960
HALF_DEV = 30
QUART_DEV = 8
CLIPS = 16
CUR = 16384
HALF = 3840
QUART = 1024
N_SEQ = 128


def draw_cur_query(key, part):
    key = jax.random.fold_in(key, 11)
    base = jnp.clip(jax.random.normal(key, (CUR, D), jnp.float32), -4.0, 4.0)
    return base.astype(jnp.bfloat16)


def draw_cur_key(key, part):
    key = jax.random.fold_in(key, 13)
    base = jnp.clip(jax.random.normal(key, (CUR, D), jnp.float32), -4.0, 4.0)
    return base.astype(jnp.bfloat16)


def block_scale(key, extent, cuts, low, largest):
    factor_of, own = 1.0, jax.random.fold_in(key, 6)
    for dim, blocks in cuts:
        draws = jnp.exp(jax.random.uniform(jax.random.fold_in(own, dim), (blocks,), jnp.float32, low / len(cuts), largest / len(cuts)))
        factor_of = factor_of * jnp.repeat(draws, extent[dim] // blocks).reshape([-1 if axis == dim else 1 for axis in range(len(extent))])
    return factor_of


def split_up(count, total, most, lean):
    loads = [(1 << 20) // math.isqrt(rank ** lean) + 1 for rank in range(2, count + 1)]
    surplus, given = total - most - (count - 1), [1] * (count - 1)
    while surplus > 0:
        movable = [i for i in range(count - 1) if given[i] < most]
        whole, left = sum([loads[i] for i in movable]), surplus
        for i in movable:
            more = min(most - given[i], max(1, left * loads[i] // whole), surplus)
            given[i] = given[i] + more
            surplus = surplus - more
    return np.array([most] + given)


def ragged_sizes(own_key, amount, total, limit, skew):
    if amount == 2:
        one = jax.random.randint(own_key, (), max(1, total - limit), min(limit, total - 1) + 1)
        return jnp.stack([one, total - one])
    sizes = jnp.asarray(split_up(amount, total, limit, skew), jnp.int32)
    pairs = (amount - 1) // 2
    donor, receiver = sizes[1:1 + 2 * pairs:2], sizes[2:2 + 2 * pairs:2]
    slack = jnp.minimum(donor - 1, limit - receiver)
    moved = jax.random.randint(jax.random.fold_in(own_key, 1), (pairs,), 0, 1 << 20) % (slack + 1)
    sizes = sizes.at[1:1 + 2 * pairs:2].set(donor - moved).at[2:2 + 2 * pairs:2].set(receiver + moved)
    return sizes[jax.random.permutation(jax.random.fold_in(own_key, 2), amount)]


def normal_values(stream_key, extent, scale, most, shards=(), held_as=jnp.bfloat16):
    values = scale * jax.random.normal(stream_key, extent, jnp.float32)
    if shards:
        values = values * block_scale(stream_key, extent, shards, -0.22, 0.18)
    return jnp.clip(values, -most, most).astype(held_as)


def setup_inputs(seed: int = 0) -> dict:
    key_list = jax.random.split(jax.random.key(seed), 12)
    cur_query = draw_cur_query(jax.random.fold_in(key_list[11], 71), 0)
    cur_key = draw_cur_key(jax.random.fold_in(key_list[11], 71), 0)
    cur_value = normal_values(key_list[2], (CUR, D), 1.0, 6.0, ((0, 128), (1, 2)))
    grad_out = normal_values(key_list[3], (CUR, D), 1.0, 6.0, ((0, 128), (1, 2)))
    out_weight = normal_values(key_list[4], (D, D), D ** -0.5, 0.15625, ((1, 2),))
    half_key = normal_values(key_list[5], (HALF, D), 1.0, 6.0, ((0, 128), (1, 2)))
    half_value = normal_values(key_list[6], (HALF, D), 1.0, 6.0, ((0, 128), (1, 2)))
    quart_key = normal_values(key_list[7], (QUART, D), 1.0, 6.0, ((0, 128), (1, 2)))
    quart_value = normal_values(key_list[8], (QUART, D), 1.0, 6.0, ((0, 128), (1, 2)))
    cur_count = jax.vmap(lambda own: ragged_sizes(own, GROUP, FRAME_TOK, C_DEV, 1))(jax.random.split(key_list[9], CLIPS)).reshape((CLIPS, GROUP)).astype(jnp.int32)
    section_bias = jnp.clip(jax.random.uniform(key_list[10], (2, HEADS), jnp.float32, -1.0, 1.0) * block_scale(key_list[10], (2, HEADS), ((1, 2),), -0.4, 0.0), -1.0, 1.0)
    return dict(cur_query=cur_query, cur_key=cur_key, cur_value=cur_value, grad_out=grad_out, out_weight=out_weight, half_key=half_key, half_value=half_value, quart_key=quart_key, quart_value=quart_value, cur_count=cur_count, section_bias=section_bias)


def lowered(values):
    return lax.optimization_barrier(values.astype(jnp.bfloat16)).astype(jnp.float32)


def reference(cur_query, cur_key, cur_value, grad_out, out_weight, half_key, half_value, quart_key, quart_value, cur_count, section_bias):
    score_scale = HD ** -0.5
    clip_total = N_SEQ // GROUP
    frame_slots = GROUP * C_DEV
    half_clip = GROUP * HALF_DEV
    quart_clip = GROUP * QUART_DEV
    key_total = frame_slots + half_clip + quart_clip
    key_bias = jnp.concatenate([jnp.zeros((frame_slots, HEADS), jnp.float32), jnp.broadcast_to(section_bias[0][None, :], (half_clip, HEADS)), jnp.broadcast_to(section_bias[1][None, :], (quart_clip, HEADS))], axis=0).T

    def clip_pass(bias_total, inputs):
        queries, keys_near, values_near, upstream, keys_half, values_half, keys_quart, values_quart, counts = inputs
        slot_valid = jnp.arange(C_DEV, dtype=jnp.int32)[None, :] < counts[:, None]
        key_valid = jnp.concatenate([slot_valid.reshape(-1), jnp.ones((half_clip + quart_clip,), dtype=bool)])
        all_keys = jnp.concatenate([keys_near.reshape(frame_slots, D), keys_half, keys_quart], axis=0).astype(jnp.float32).reshape(key_total, HEADS, HD)
        all_values = jnp.concatenate([values_near.reshape(frame_slots, D), values_half, values_quart], axis=0).astype(jnp.float32).reshape(key_total, HEADS, HD)

        def shard_pass(carry, shard_inputs):
            key_acc, value_acc, bias_acc = carry
            query_rows, upstream_rows, valid_rows = shard_inputs
            upstream_rows = jnp.where(valid_rows[:, None], upstream_rows, jnp.zeros_like(upstream_rows))
            query_heads = query_rows.astype(jnp.float32).reshape(C_DEV, HEADS, HD)
            scores = jnp.einsum('qhd,khd->hqk', query_heads, all_keys) * score_scale
            scores = scores + key_bias[:, None, :]
            scores = jnp.where(key_valid[None, None, :], scores, jnp.float32(-1e30))
            row_top = jnp.max(scores, axis=2, keepdims=True)
            exponent = jnp.exp(scores - row_top)
            softmax_probs = exponent / jnp.sum(exponent, axis=2, keepdims=True)
            probs_low = lowered(softmax_probs)
            attn_rows = jnp.einsum('hqk,khd->qhd', probs_low, all_values).reshape(C_DEV, D).astype(jnp.bfloat16)
            adjoint = jnp.dot(upstream_rows, out_weight, preferred_element_type=jnp.float32).astype(jnp.bfloat16)
            adjoint_heads = adjoint.astype(jnp.float32).reshape(C_DEV, HEADS, HD)
            attn_heads = attn_rows.astype(jnp.float32).reshape(C_DEV, HEADS, HD)
            d_prob = jnp.einsum('qhd,khd->hqk', adjoint_heads, all_values)
            row_delta = jnp.sum(adjoint_heads * attn_heads, axis=2).T[:, :, None]
            d_score = softmax_probs * (d_prob - row_delta)
            score_low = lowered(d_score)
            query_grad = (jnp.einsum('hqk,khd->qhd', score_low, all_keys) * score_scale).reshape(C_DEV, D).astype(jnp.bfloat16)
            key_grad = (jnp.einsum('hqk,qhd->khd', score_low, query_heads) * score_scale).reshape(key_total, D)
            value_grad = jnp.einsum('hqk,qhd->khd', probs_low, adjoint_heads).reshape(key_total, D)
            key_sums = jnp.sum(d_score, axis=1)
            half_term = jnp.sum(key_sums[:, frame_slots:frame_slots + half_clip], axis=1)
            quart_term = jnp.sum(key_sums[:, frame_slots + half_clip:], axis=1)
            carry = (key_acc + lowered(key_grad), value_acc + lowered(value_grad), bias_acc + jnp.stack([half_term, quart_term]))
            return carry, query_grad

        start = (jnp.zeros((key_total, D), jnp.float32), jnp.zeros((key_total, D), jnp.float32), jnp.zeros((2, HEADS), jnp.float32))
        finals, query_grads = lax.scan(shard_pass, start, (queries, upstream, slot_valid))
        key_acc, value_acc, bias_acc = finals
        outs = (query_grads.reshape(frame_slots, D),
                key_acc[:frame_slots].astype(jnp.bfloat16), value_acc[:frame_slots].astype(jnp.bfloat16),
                key_acc[frame_slots:frame_slots + half_clip].astype(jnp.bfloat16), value_acc[frame_slots:frame_slots + half_clip].astype(jnp.bfloat16),
                key_acc[frame_slots + half_clip:].astype(jnp.bfloat16), value_acc[frame_slots + half_clip:].astype(jnp.bfloat16))
        return bias_total + bias_acc, outs

    inputs = (cur_query.reshape(clip_total, GROUP, C_DEV, D), cur_key.reshape(clip_total, GROUP, C_DEV, D),
              cur_value.reshape(clip_total, GROUP, C_DEV, D), grad_out.reshape(clip_total, GROUP, C_DEV, D),
              half_key.reshape(clip_total, half_clip, D), half_value.reshape(clip_total, half_clip, D),
              quart_key.reshape(clip_total, quart_clip, D), quart_value.reshape(clip_total, quart_clip, D), cur_count)
    bias_total, outs = lax.scan(clip_pass, jnp.zeros((2, HEADS), jnp.float32), inputs)
    d_query = outs[0].reshape(CUR, D)
    d_key = outs[1].reshape(CUR, D)
    d_value = outs[2].reshape(CUR, D)
    d_half_key = outs[3].reshape(HALF, D)
    d_half_value = outs[4].reshape(HALF, D)
    d_quart_key = outs[5].reshape(QUART, D)
    d_quart_value = outs[6].reshape(QUART, D)
    return (d_query, d_key, d_value, d_half_key, d_half_value, d_quart_key, d_quart_value, bias_total)
```

```python
import functools

import jax
import jax.numpy as jnp
from jax import lax
from jax.experimental import pallas as pl
from jax.experimental.pallas import tpu as pltpu
from jax.sharding import PartitionSpec as P

HD = 64
LANES = 128
CHIPS = 4
HEADS = 3
MESH = pl.DeviceIdType.MESH
BF = jnp.bfloat16
F32 = jnp.float32


def dot(a, b, ca, cb):
    return lax.dot_general(a, b, (((ca,), (cb,)), ((), ())), preferred_element_type=F32)


def joined(a, b, upper):
    if upper:
        return jnp.concatenate([a[:, HD:], b[:, HD:]], axis=1)
    return jnp.concatenate([a[:, :HD], b[:, :HD]], axis=1)


def exchange_kernel(
    n_x,
    n_z,
    query_hbm,
    key_hbm,
    value_hbm,
    grad_hbm,
    weight_hbm,
    half_key,
    half_value,
    quart_key,
    quart_value,
    counts,
    section_bias,
    dq_out,
    dkv_out,
    bias_out,
    query,
    key,
    value,
    grad,
    grad_far,
    weight,
    kv_send,
    qa_send,
    kv_all,
    qa_all,
    count_bias,
    key_bias,
    scores,
    d_probs,
    low,
    part_send,
    part_got,
    own_sum,
    dkv_send,
    dq_send,
    bias_send,
    bias_clip,
    bias_x,
    bias_z,
    load_sem,
    z_sem,
    kv_ss,
    kv_rs,
    sib_ss,
    sib_rs,
    fwd_ss,
    fwd_rs,
    qa_ss,
    qa_rs,
    part_ss,
    part_rs,
    dkv_ss,
    dkv_rs,
    dq_ss,
    dq_rs,
    clip_ss,
    clip_rs,
    x_ss,
    x_rs,
    zz_ss,
    zz_rs,
):
    rows = query_hbm.shape[0]
    half_rows = half_key.shape[0]
    quart_rows = quart_key.shape[0]
    width = query_hbm.shape[1]
    block = kv_send.shape[1]
    quart_at = block - 16
    heads = width // HD
    seq = lax.axis_index("seq")
    head = lax.axis_index("head")
    core = seq % 2
    y = seq // 2 % CHIPS
    z = seq // 8 % n_z
    x = seq // (8 * n_z)
    clip = seq // 8

    def device(x, z, y, core):
        return ((x * n_z + z) * CHIPS + y) * 2 + core

    def chip(dy):
        return (y + dy) % CHIPS

    def copy(src, dst, ss, rs, seq_to, head_to=None):
        return pltpu.make_async_remote_copy(
            src_ref=src,
            dst_ref=dst,
            send_sem=ss,
            recv_sem=rs,
            device_id={"seq": seq_to, "head": head if head_to is None else head_to},
            device_id_type=MESH,
        )

    loads = [
        pltpu.make_async_copy(a, b, load_sem.at[i])
        for i, (a, b) in enumerate(
            [
                (key_hbm, key),
                (value_hbm, value),
                (grad_hbm, grad),
                (query_hbm, query),
                (weight_hbm, weight),
            ]
        )
    ]
    for load in loads:
        load.start()

    sibling = device(x, z, y, 1 - core)
    partners = [(device(x, z, chip(dy), c), head) for dy in range(CHIPS) for c in (core, 1 - core)][1:]
    partners += [(device((x + d) % n_x, z, y, core), head) for d in range(1, n_x)]
    partners += [(device(x, (z + d) % n_z, y, core), head) for d in range(1, n_z)]
    partners += [(seq, 1 - head)]
    barrier = pltpu.get_barrier_semaphore()
    for seq_to, head_to in partners:
        pl.semaphore_signal(
            barrier, inc=1, device_id={"seq": seq_to, "head": head_to}, device_id_type=MESH
        )

    loads[0].wait()
    loads[1].wait()
    zeros = jnp.zeros((block - rows, LANES), BF)
    for i in range(heads // 2):
        cols = slice(i * LANES, (i + 1) * LANES)
        for upper in (False, True):
            at = 2 * i + upper
            kv_send[at, :rows] = joined(key[:, cols], value[:, cols], upper)
            kv_send[at, rows:] = zeros
            kv_send[at, rows : rows + half_rows] = joined(
                half_key[:, cols], half_value[:, cols], upper
            )
            kv_send[at, quart_at : quart_at + quart_rows] = joined(
                quart_key[:, cols], quart_value[:, cols], upper
            )

    pl.semaphore_wait(barrier, len(partners))

    z_copy = copy(grad_hbm, grad_far, z_sem.at[0], z_sem.at[1], seq, 1 - head)
    z_copy.start()
    kv_copies = {}
    sib_copies = []
    for j in range(HEADS):
        for dy in (1, 3, 2):
            c = copy(
                kv_send.at[HEADS * chip(dy) + j],
                kv_all.at[j, 0, dy],
                kv_ss.at[j, dy],
                kv_rs.at[j, dy],
                device(x, z, chip(dy), core),
            )
            c.start()
            kv_copies[j, dy] = c
        c = copy(
            kv_send.at[HEADS * y + j], kv_all.at[j, 1, 0], sib_ss.at[j], sib_rs.at[j], sibling
        )
        c.start()
        sib_copies.append(c)
        kv_all[j, 0, 0] = kv_send[HEADS * y + j]

    row_id = lax.broadcasted_iota(jnp.int32, (rows, LANES), 0)
    for c in range(2 * CHIPS):
        p, dy = divmod(c, CHIPS)
        shard = 2 * chip(CHIPS - dy) + (core if p == 0 else 1 - core)
        count_bias[c] = jnp.where(row_id < counts[clip, shard], F32(0), F32(-1e30))

    loads[2].wait()
    loads[4].wait()
    adjoint = dot(grad[...], weight[pl.ds(pl.multiple_of(head * width, LANES), width), :], 1, 0)

    fwd_copies = {}

    def forward(j):
        for dy in (1, 3, 2):
            kv_copies[j, dy].wait_recv()
            c = copy(
                kv_all.at[j, 0, dy],
                kv_all.at[j, 1, dy],
                fwd_ss.at[j, dy],
                fwd_rs.at[j, dy],
                sibling,
            )
            c.start()
            fwd_copies[j, dy] = c

    forward(0)
    forward(1)
    loads[3].wait()
    z_copy.wait()
    adjoint += dot(
        grad_far[...], weight[pl.ds(pl.multiple_of((1 - head) * width, LANES), width), :], 1, 0
    )
    own_count = counts[clip, 2 * y + core]
    row_wide = lax.broadcasted_iota(jnp.int32, (rows, width), 0)
    adjoint = jnp.where(row_wide < own_count, adjoint, F32(0)).astype(BF)
    for i in range(heads // 2):
        cols = slice(i * LANES, (i + 1) * LANES)
        scaled = query[:, cols] * BF(HD**-0.5)
        for upper in (False, True):
            qa_send[2 * i + upper] = joined(scaled, adjoint[:, cols], upper)
    qa_copies = {}
    for j in range(HEADS):
        for dy in (1, 3, 2):
            c = copy(
                qa_send.at[HEADS * chip(dy) + j],
                qa_all.at[j, dy],
                qa_ss.at[j, dy],
                qa_rs.at[j, dy],
                device(x, z, chip(dy), core),
            )
            c.start()
            qa_copies[j, dy] = c
        qa_all[j, 0] = qa_send[HEADS * y + j]
    forward(2)

    bias_row = lax.broadcasted_iota(jnp.int32, (8, LANES), 0)
    bias_lane = lax.broadcasted_iota(jnp.int32, (8, LANES), 1)
    hist_id = lax.broadcasted_iota(jnp.int32, (block - rows, LANES), 0)
    queries = CHIPS * rows
    groups = queries // LANES
    lane_id = lax.broadcasted_iota(jnp.int32, (queries, LANES), 1)

    def fold(t, op):
        total = t[:8]
        for r in range(8, t.shape[0], 8):
            total = op(total, t[r : r + 8])
        return total

    bias_total = jnp.zeros((8, LANES), F32)
    out_copies = []
    for j in range(HEADS):
        for dy in (1, 3, 2):
            qa_copies[j, dy].wait_recv()
            fwd_copies[j, dy].wait_recv()
        sib_copies[j].wait_recv()
        my_head = HEADS * y + j
        half_bias = section_bias[0, my_head]
        quart_bias = section_bias[1, my_head]
        hist_bias = jnp.where(
            hist_id < half_rows,
            half_bias,
            jnp.where(
                (hist_id >= quart_at - rows) & (hist_id < quart_at - rows + quart_rows),
                quart_bias,
                F32(-1e30),
            ),
        )
        qa = qa_all[j].reshape(queries, LANES)
        q_part = jnp.where(lane_id < HD, qa, BF(0))
        a_part = jnp.where(lane_id < HD, BF(0), qa)
        top = jnp.full((8, queries), -3e38, F32)
        for c in range(2 * CHIPS):
            s = dot(kv_all[j, c // CHIPS, c % CHIPS], q_part, 1, 1)
            bias = jnp.concatenate([count_bias[c], hist_bias], axis=0)
            s = s + jnp.concatenate([bias] * groups, axis=1)
            scores[c] = s
            top = jnp.maximum(top, fold(s, jnp.maximum))
        top = jnp.max(top, axis=0, keepdims=True)
        total = jnp.zeros((8, queries), F32)
        delta = jnp.zeros((8, queries), F32)
        for c in range(2 * CHIPS):
            dp = dot(kv_all[j, c // CHIPS, c % CHIPS], a_part, 1, 1)
            e = jnp.exp(scores[c] - top)
            scores[c] = e
            d_probs[c] = dp
            total = total + fold(e, jnp.add)
            delta = delta + fold(e * dp, jnp.add)
        inverse = 1.0 / jnp.sum(total, axis=0, keepdims=True)
        delta = jnp.sum(delta, axis=0, keepdims=True) * inverse
        both = jnp.concatenate([q_part, a_part], axis=0)
        half_sum = jnp.zeros((8, queries), F32)
        quart_sum = jnp.zeros((8, queries), F32)
        for c in list(range(CHIPS, 2 * CHIPS)) + list(range(CHIPS)):
            probs = scores[c] * inverse
            ds = probs * (d_probs[c] - delta)
            half_sum = half_sum + fold(ds[rows:quart_at], jnp.add)
            quart_sum = quart_sum + fold(ds[quart_at:], jnp.add)
            ds_low = ds.astype(BF)
            low[c * block : (c + 1) * block] = ds_low
            part = dot(jnp.concatenate([ds_low, probs.astype(BF)], axis=1), both, 1, 0)
            if c >= CHIPS:
                part_send[j, c - CHIPS] = part.astype(BF)
            else:
                own_sum[c] = part
            if c == 2 * CHIPS - 1:
                part_copy = copy(
                    part_send.at[j], part_got.at[j], part_ss.at[j], part_rs.at[j], sibling
                )
                part_copy.start()
        bias_total = jnp.where(
            bias_lane == my_head,
            jnp.where(bias_row == 0, jnp.sum(half_sum), jnp.sum(quart_sum)),
            bias_total,
        )
        kv = kv_all[j].reshape(2 * CHIPS * block, LANES)
        dq = (dot(kv, low[...], 0, 0)[:HD] * F32(HD**-0.5)).astype(BF)
        for dy in range(CHIPS):
            dq_send[j, dy] = dq[:, dy * rows : (dy + 1) * rows]
        dq_out[my_head] = dq[:, :rows]
        for dy in (1, 3, 2):
            c = copy(
                dq_send.at[j, dy],
                dq_out.at[my_head],
                dq_ss.at[j, dy],
                dq_rs.at[j, dy],
                device(x, z, chip(CHIPS - dy), core),
            )
            c.start()
            out_copies.append(c)
        part_copy.wait()
        for dy in (1, 3, 2, 0):
            done = (own_sum[dy] + part_got[j, dy].astype(F32)).astype(BF)
            if dy == 0:
                dkv_out[my_head] = done
                continue
            dkv_send[j, dy] = done
            c = copy(
                dkv_send.at[j, dy],
                dkv_out.at[my_head],
                dkv_ss.at[j, dy],
                dkv_rs.at[j, dy],
                device(x, z, chip(CHIPS - dy), core),
            )
            c.start()
            out_copies.append(c)

    bias_send[0] = bias_total
    copies = []
    for i in range(1, 2 * CHIPS):
        dy, p = divmod(i, 2)
        c = copy(
            bias_send.at[0],
            bias_clip.at[i],
            clip_ss.at[i],
            clip_rs.at[i],
            device(x, z, chip(dy), (core + p) % 2),
        )
        c.start()
        copies.append(c)
    for c in copies:
        c.wait()
    for i in range(1, 2 * CHIPS):
        bias_total = bias_total + bias_clip[i]

    def spread(total, count, me, at, slots, stage, ss, rs):
        if count == 1:
            return total
        bias_send[stage] = total
        slots[me] = total
        copies = []
        for d in range(1, count):
            c = copy(
                bias_send.at[stage], slots.at[me], ss.at[d], rs.at[d], at((me + d) % count)
            )
            c.start()
            copies.append(c)
        for c in copies:
            c.wait()
        total = slots[0]
        for d in range(1, count):
            total = total + slots[d]
        return total

    bias_total = spread(
        bias_total, n_x, x, lambda i: device(i, z, y, core), bias_x, 1, x_ss, x_rs
    )
    bias_total = spread(
        bias_total, n_z, z, lambda i: device(x, i, y, core), bias_z, 2, zz_ss, zz_rs
    )
    bias_out[...] = bias_total

    for c in kv_copies.values():
        c.wait_send()
    for c in sib_copies:
        c.wait_send()
    for c in fwd_copies.values():
        c.wait_send()
    for c in qa_copies.values():
        c.wait_send()
    for c in out_copies:
        c.wait()


def finish_kernel(
    half_rows,
    quart_rows,
    dq,
    dkv,
    bias,
    d_query,
    d_key,
    d_value,
    d_half_key,
    d_half_value,
    d_quart_key,
    d_quart_value,
    d_bias,
):
    heads = dq.shape[0]
    rows = d_key.shape[0]
    quart_at = dkv.shape[1] - 16
    for i in range(heads // 2):
        cols = slice(i * LANES, (i + 1) * LANES)
        d_query[:, cols] = dq[2 * i : 2 * i + 2].reshape(LANES, rows).T
        low, high = dkv[2 * i], dkv[2 * i + 1]
        for upper, outs in (
            (False, (d_key, d_half_key, d_quart_key)),
            (True, (d_value, d_half_value, d_quart_value)),
        ):
            both = joined(low, high, upper)
            outs[0][:, cols] = both[:rows]
            outs[1][:, cols] = both[rows : rows + half_rows]
            outs[2][:, cols] = both[quart_at : quart_at + quart_rows]
    d_bias[...] = bias[: d_bias.shape[0], : d_bias.shape[1]]


def shards(
    cur_query,
    cur_key,
    cur_value,
    grad_out,
    out_weight,
    half_key,
    half_value,
    quart_key,
    quart_value,
    cur_count,
    section_bias,
    n_x,
    n_z,
):
    rows, width = cur_query.shape
    half_rows, quart_rows = half_key.shape[0], quart_key.shape[0]
    heads = width // HD
    block = rows + 48
    anywhere = pl.BlockSpec(memory_space=pl.ANY)
    vmem = pl.BlockSpec(memory_space=pltpu.VMEM)
    smem = pl.BlockSpec(memory_space=pltpu.SMEM)
    dma = pltpu.SemaphoreType.DMA
    queries = CHIPS * rows
    shards_n = 2 * CHIPS
    pair = [dma((HEADS, CHIPS)), dma((HEADS, CHIPS))]
    triple = [dma((HEADS,)), dma((HEADS,))]
    dq, dkv, bias = pl.pallas_call(
        functools.partial(exchange_kernel, n_x, n_z),
        out_shape=(
            jax.ShapeDtypeStruct((heads, HD, rows), BF),
            jax.ShapeDtypeStruct((heads, block, LANES), BF),
            jax.ShapeDtypeStruct((8, LANES), F32),
        ),
        in_specs=[anywhere] * 5 + [vmem] * 4 + [smem] * 2,
        out_specs=(vmem, vmem, vmem),
        scratch_shapes=[
            pltpu.VMEM((rows, width), BF),
            pltpu.VMEM((rows, width), BF),
            pltpu.VMEM((rows, width), BF),
            pltpu.VMEM((rows, width), BF),
            pltpu.VMEM((rows, width), BF),
            pltpu.VMEM(out_weight.shape, BF),
            pltpu.VMEM((heads, block, LANES), BF),
            pltpu.VMEM((heads, rows, LANES), BF),
            pltpu.VMEM((HEADS, 2, CHIPS, block, LANES), BF),
            pltpu.VMEM((HEADS, CHIPS, rows, LANES), BF),
            pltpu.VMEM((shards_n, rows, LANES), F32),
            pltpu.VMEM((8, LANES), F32),
            pltpu.VMEM((shards_n, block, queries), F32),
            pltpu.VMEM((shards_n, block, queries), F32),
            pltpu.VMEM((shards_n * block, queries), BF),
            pltpu.VMEM((HEADS, CHIPS, block, LANES), BF),
            pltpu.VMEM((HEADS, CHIPS, block, LANES), BF),
            pltpu.VMEM((CHIPS, block, LANES), F32),
            pltpu.VMEM((HEADS, CHIPS, block, LANES), BF),
            pltpu.VMEM((HEADS, CHIPS, HD, rows), BF),
            pltpu.VMEM((3, 8, LANES), F32),
            pltpu.VMEM((shards_n, 8, LANES), F32),
            pltpu.VMEM((n_x, 8, LANES), F32),
            pltpu.VMEM((n_z, 8, LANES), F32),
            dma((5,)),
            dma((2,)),
            *pair,
            *triple,
            *pair,
            *pair,
            *triple,
            *pair,
            *pair,
            dma((shards_n,)),
            dma((shards_n,)),
            dma((n_x,)),
            dma((n_x,)),
            dma((n_z,)),
            dma((n_z,)),
        ],
        compiler_params=pltpu.CompilerParams(
            collective_id=0, has_side_effects=True, vmem_limit_bytes=48 << 20
        ),
        name="exchange",
    )(
        cur_query,
        cur_key,
        cur_value,
        grad_out,
        out_weight,
        half_key,
        half_value,
        quart_key,
        quart_value,
        cur_count,
        section_bias,
    )
    like = lambda a: jax.ShapeDtypeStruct(a.shape, a.dtype)
    return pl.pallas_call(
        functools.partial(finish_kernel, half_rows, quart_rows),
        out_shape=(
            like(cur_query),
            like(cur_key),
            like(cur_value),
            like(half_key),
            like(half_value),
            like(quart_key),
            like(quart_value),
            like(section_bias),
        ),
        in_specs=[vmem] * 3,
        out_specs=(vmem,) * 8,
        name="finish",
    )(dq, dkv, bias)


def solution(mesh):
    n_z = 4
    n_x = mesh.shape["seq"] // (2 * CHIPS * n_z)
    return jax.shard_map(
        functools.partial(shards, n_x=n_x, n_z=n_z),
        mesh=mesh,
        in_specs=(
            P("seq", "head"),
            P("seq", "head"),
            P("seq", "head"),
            P("seq", "head"),
            P(None, "head"),
            P("seq", "head"),
            P("seq", "head"),
            P("seq", "head"),
            P("seq", "head"),
            P(),
            P(None, "head"),
        ),
        out_specs=(
            P("seq", "head"),
            P("seq", "head"),
            P("seq", "head"),
            P("seq", "head"),
            P("seq", "head"),
            P("seq", "head"),
            P("seq", "head"),
            P(None, "head"),
        ),
        check_vma=False,
    )
```

```python
import functools

import jax
import jax.numpy as jnp
from jax import lax
from jax.experimental import pallas as pl
from jax.experimental.pallas import tpu as pltpu
from jax.sharding import PartitionSpec as P

HD = 64
LANES = 128
CHIPS = 4
HEADS = 3
FAR = 3
MESH = pl.DeviceIdType.MESH
BF = jnp.bfloat16
F32 = jnp.float32


def dot(a, b, ca, cb):
    return lax.dot_general(a, b, (((ca,), (cb,)), ((), ())), preferred_element_type=F32)


def joined(a, head_a, b, head_b):
    return jnp.concatenate(
        [a[:, head_a * HD : (head_a + 1) * HD], b[:, head_b * HD : (head_b + 1) * HD]], axis=1
    )


def exchange_kernel(
    n_x,
    n_z,
    query_hbm,
    key_hbm,
    value_hbm,
    grad_hbm,
    weight_hbm,
    half_key_hbm,
    half_value_hbm,
    quart_key_hbm,
    quart_value_hbm,
    counts_hbm,
    section_bias_hbm,
    dq_out,
    dkv_out,
    bias_out,
    query,
    key,
    value,
    grad,
    grad_far,
    weight,
    half_key,
    half_value,
    quart_key,
    quart_value,
    counts,
    section_bias,
    kv_send,
    qa_send,
    kv_all,
    qa_all,
    count_bias,
    tops,
    scores,
    d_probs,
    low,
    part_send,
    part_got,
    own_sum,
    dkv_send,
    dq_send,
    bias_send,
    bias_zc,
    bias_xy,
    load_sem,
    z_ss,
    z_rs,
    kv_ss,
    kv_rs,
    sib_ss,
    sib_rs,
    fwd_ss,
    fwd_rs,
    qa_ss,
    qa_rs,
    part_ss,
    part_rs,
    dkv_ss,
    dkv_rs,
    dq_ss,
    dq_rs,
    zc_ss,
    zc_rs,
    xy_ss,
    xy_rs,
):
    rows = query_hbm.shape[0]
    half_rows = half_key_hbm.shape[0]
    quart_rows = quart_key_hbm.shape[0]
    width = query_hbm.shape[1]
    block = kv_send.shape[1]
    quart_at = block - 16
    heads = width // HD
    seq = lax.axis_index("seq")
    head = lax.axis_index("head")
    core = seq % 2
    y = seq // 2 % CHIPS
    z = seq // 8 % n_z
    x = seq // (8 * n_z)
    clip = seq // 8

    def device(x, z, y, core):
        return ((x * n_z + z) * CHIPS + y) * 2 + core

    def chip(dy):
        return (y + dy) % CHIPS

    def copy(src, dst, ss, rs, seq_to, head_to=None):
        return pltpu.make_async_remote_copy(
            src_ref=src,
            dst_ref=dst,
            send_sem=ss,
            recv_sem=rs,
            device_id={"seq": seq_to, "head": head if head_to is None else head_to},
            device_id_type=MESH,
        )

    loads = [
        pltpu.make_async_copy(a, b, load_sem.at[i])
        for i, (a, b) in enumerate(
            [
                (query_hbm, query),
                (key_hbm, key),
                (value_hbm, value),
                (half_key_hbm, half_key),
                (half_value_hbm, half_value),
                (quart_key_hbm, quart_key),
                (quart_value_hbm, quart_value),
                (counts_hbm, counts),
                (section_bias_hbm, section_bias),
                (grad_hbm, grad),
                (weight_hbm, weight),
            ]
        )
    ]
    for load in loads:
        load.start()

    sibling = device(x, z, y, 1 - core)
    zc_peers = [
        device(x, (z + d) % n_z, y, (core + p) % 2) for d in range(n_z) for p in range(2)
    ][1:]
    xy_peers = [device((x + d) % n_x, z, chip(dy), core) for d in range(n_x) for dy in range(CHIPS)][1:]
    partners = [(seq, 1 - head)] + [(peer, head) for peer in zc_peers + xy_peers]
    barrier = pltpu.get_barrier_semaphore()
    for seq_to, head_to in partners:
        pl.semaphore_signal(
            barrier, inc=1, device_id={"seq": seq_to, "head": head_to}, device_id_type=MESH
        )

    for load in loads[:7]:
        load.wait()
    zeros = jnp.zeros((block - rows, LANES), BF)
    for h in range(heads):
        first, second = (value, key) if h % HEADS == 1 else (key, value)
        kv_send[h, :rows] = joined(first, h, second, h)
        kv_send[h, rows:] = zeros
        first, second = (half_value, half_key) if h % HEADS == 1 else (half_key, half_value)
        kv_send[h, rows : rows + half_rows] = joined(first, h, second, h)
        first, second = (quart_value, quart_key) if h % HEADS == 1 else (quart_key, quart_value)
        kv_send[h, quart_at : quart_at + quart_rows] = joined(first, h, second, h)
    query[...] = query[...] * BF(HD**-0.5)
    for c in range(CHIPS):
        qa_send[HEADS * c] = joined(query, HEADS * c, query, HEADS * c + 1)

    pl.semaphore_wait(barrier, len(partners))

    far_cols = width // FAR
    z_copies = []
    for i in range(FAR):
        cols = slice(i * far_cols, (i + 1) * far_cols)
        c = copy(
            grad_hbm.at[:, cols], grad_far.at[:, cols], z_ss.at[i], z_rs.at[i], seq, 1 - head
        )
        c.start()
        z_copies.append(c)
    qa_copies = {}

    def send_tile(t):
        for dy in (1, 3, 2):
            c = copy(
                qa_send.at[HEADS * chip(dy) + t],
                qa_all.at[t, dy],
                qa_ss.at[t, dy],
                qa_rs.at[t, dy],
                device(x, z, chip(dy), core),
            )
            c.start()
            qa_copies[t, dy] = c
        qa_all[t, 0] = qa_send[HEADS * y + t]

    send_tile(0)
    kv_copies = {}
    sib_copies = []
    for j in range(HEADS):
        for dy in (1, 3, 2):
            c = copy(
                kv_send.at[HEADS * chip(dy) + j],
                kv_all.at[j, 0, dy],
                kv_ss.at[j, dy],
                kv_rs.at[j, dy],
                device(x, z, chip(dy), core),
            )
            c.start()
            kv_copies[j, dy] = c
        c = copy(
            kv_send.at[HEADS * y + j], kv_all.at[j, 1, 0], sib_ss.at[j], sib_rs.at[j], sibling
        )
        c.start()
        sib_copies.append(c)
        kv_all[j, 0, 0] = kv_send[HEADS * y + j]

    loads[7].wait()
    loads[8].wait()
    row_id = lax.broadcasted_iota(jnp.int32, (rows, LANES), 0)
    for c in range(2 * CHIPS):
        p, dy = divmod(c, CHIPS)
        shard = 2 * chip(CHIPS - dy) + (core if p == 0 else 1 - core)
        count_bias[c] = jnp.where(row_id < counts[shard, clip], F32(0), F32(-1e30))

    loads[9].wait()
    loads[10].wait()
    adjoint = dot(grad[...], weight[pl.ds(pl.multiple_of(head * width, LANES), width), :], 1, 0)

    fwd_copies = {}

    def forward(j):
        for dy in (1, 3, 2):
            kv_copies[j, dy].wait_recv()
            c = copy(
                kv_all.at[j, 0, dy],
                kv_all.at[j, 1, dy],
                fwd_ss.at[j, dy],
                fwd_rs.at[j, dy],
                sibling,
            )
            c.start()
            fwd_copies[j, dy] = c

    forward(0)
    forward(1)
    for i in range(FAR):
        z_copies[i].wait_recv()
        at = pl.multiple_of((1 - head) * width + i * far_cols, LANES)
        adjoint += dot(
            grad_far[:, i * far_cols : (i + 1) * far_cols], weight[pl.ds(at, far_cols), :], 1, 0
        )
    own_count = counts[2 * y + core, clip]
    row_wide = lax.broadcasted_iota(jnp.int32, (rows, width), 0)
    adjoint = jnp.where(row_wide < own_count, adjoint, F32(0)).astype(BF)
    for c in range(CHIPS):
        qa_send[HEADS * c + 1] = joined(adjoint, HEADS * c + 1, adjoint, HEADS * c)
    send_tile(1)
    for c in range(CHIPS):
        qa_send[HEADS * c + 2] = joined(query, HEADS * c + 2, adjoint, HEADS * c + 2)
    send_tile(2)
    forward(2)

    bias_row = lax.broadcasted_iota(jnp.int32, (8, LANES), 0)
    bias_lane = lax.broadcasted_iota(jnp.int32, (8, LANES), 1)
    hist_id = lax.broadcasted_iota(jnp.int32, (block - rows, LANES), 0)
    queries = CHIPS * rows
    groups = queries // LANES
    low_lane = lax.broadcasted_iota(jnp.int32, (queries, LANES), 1) < HD

    def fold(t, op):
        total = t[:8]
        for r in range(8, t.shape[0], 8):
            total = op(total, t[r : r + 8])
        return total

    def wait_tile(t):
        for dy in (1, 3, 2):
            qa_copies[t, dy].wait_recv()

    def wait_keys(j):
        for dy in (1, 3, 2):
            fwd_copies[j, dy].wait_recv()
        sib_copies[j].wait_recv()

    def query_part(j):
        tile = qa_all[2 if j == 2 else 0].reshape(queries, LANES)
        return jnp.where(low_lane, BF(0), tile) if j == 1 else jnp.where(low_lane, tile, BF(0))

    def adjoint_part(j):
        tile = qa_all[2 if j == 2 else 1].reshape(queries, LANES)
        return jnp.where(low_lane, tile, BF(0)) if j == 1 else jnp.where(low_lane, BF(0), tile)

    def score_pass(j):
        my_head = HEADS * y + j
        half_bias = section_bias[0, my_head]
        quart_bias = section_bias[1, my_head]
        hist_bias = jnp.where(
            hist_id < half_rows,
            half_bias,
            jnp.where(
                (hist_id >= quart_at - rows) & (hist_id < quart_at - rows + quart_rows),
                quart_bias,
                F32(-1e30),
            ),
        )
        q_part = query_part(j)
        top = jnp.full((8, queries), -3e38, F32)
        for c in range(2 * CHIPS):
            s = dot(kv_all[j, c // CHIPS, c % CHIPS], q_part, 1, 1)
            bias = jnp.concatenate([count_bias[c], hist_bias], axis=0)
            s = s + jnp.concatenate([bias] * groups, axis=1)
            scores[j, c] = s
            top = jnp.maximum(top, fold(s, jnp.maximum))
        tops[j] = top

    def dscore_pass(j):
        a_part = adjoint_part(j)
        top = jnp.max(tops[j], axis=0, keepdims=True)
        total = jnp.zeros((8, queries), F32)
        delta = jnp.zeros((8, queries), F32)
        for c in range(2 * CHIPS):
            dp = dot(kv_all[j, c // CHIPS, c % CHIPS], a_part, 1, 1)
            e = jnp.exp(scores[j, c] - top)
            scores[j, c] = e
            d_probs[c] = dp
            total = total + fold(e, jnp.add)
            delta = delta + fold(e * dp, jnp.add)
        inverse = 1.0 / jnp.sum(total, axis=0, keepdims=True)
        delta = jnp.sum(delta, axis=0, keepdims=True) * inverse
        half_sum = jnp.zeros((8, queries), F32)
        quart_sum = jnp.zeros((8, queries), F32)
        for c in range(2 * CHIPS):
            probs = scores[j, c] * inverse
            ds = probs * (d_probs[c] - delta)
            half_sum = half_sum + fold(ds[rows:quart_at], jnp.add)
            quart_sum = quart_sum + fold(ds[quart_at:], jnp.add)
            low[j, c * block : (c + 1) * block, :queries] = ds.astype(BF)
            low[j, c * block : (c + 1) * block, queries:] = probs.astype(BF)
        return jnp.where(
            bias_lane == HEADS * y + j,
            jnp.where(bias_row == 0, jnp.sum(half_sum), jnp.sum(quart_sum)),
            F32(0),
        )

    part_copies = {}
    out_copies = []
    own_copies = []

    def products(j):
        my_head = HEADS * y + j
        near = CHIPS * block
        both = jnp.concatenate([query_part(j), adjoint_part(j)], axis=0)
        kv = kv_all[j].reshape(2 * near, LANES)
        at = HD if j == 1 else 0
        dq = (dot(kv, low[j, :, :queries], 0, 0)[at : at + HD] * F32(HD**-0.5)).astype(BF)
        for dy in range(CHIPS):
            dq_send[j, dy] = dq[:, dy * rows : (dy + 1) * rows]
        for dy in (1, 3, 2):
            c = copy(
                dq_send.at[j, dy],
                dq_out.at[my_head],
                dq_ss.at[j, dy],
                dq_rs.at[j, dy],
                device(x, z, chip(CHIPS - dy), core),
            )
            c.start()
            out_copies.append(c)
        c = pltpu.make_async_copy(dq_send.at[j, 0], dq_out.at[my_head], dq_ss.at[j, 0])
        c.start()
        own_copies.append(c)
        part_send[j] = dot(low[j, near:], both, 1, 0).astype(BF)
        c = copy(part_send.at[j], part_got.at[j], part_ss.at[j], part_rs.at[j], sibling)
        c.start()
        part_copies[j] = c
        own_sum[j] = dot(low[j, :near], both, 1, 0)

    def send_keys(j):
        my_head = HEADS * y + j
        part_copies[j].wait()
        for dy in (1, 3, 2, 0):
            at = slice(dy * block, (dy + 1) * block)
            dkv_send[j, dy] = (own_sum[j, at] + part_got[j, at].astype(F32)).astype(BF)
            if dy == 0:
                c = pltpu.make_async_copy(dkv_send.at[j, 0], dkv_out.at[my_head], dkv_ss.at[j, 0])
                c.start()
                own_copies.append(c)
                continue
            c = copy(
                dkv_send.at[j, dy],
                dkv_out.at[my_head],
                dkv_ss.at[j, dy],
                dkv_rs.at[j, dy],
                device(x, z, chip(CHIPS - dy), core),
            )
            c.start()
            out_copies.append(c)

    def spread(total, stage, peers, slots, me, ss, rs):
        bias_send[stage] = total
        slots[me] = total
        copies = []
        for i, peer in enumerate(peers):
            c = copy(bias_send.at[stage], slots.at[me], ss.at[i], rs.at[i], peer)
            c.start()
            copies.append(c)
        return copies

    def gathered(slots, copies):
        for c in copies:
            c.wait()
        total = slots[0]
        for i in range(1, len(copies) + 1):
            total = total + slots[i]
        return total

    wait_tile(0)
    wait_keys(0)
    score_pass(0)
    wait_keys(1)
    score_pass(1)
    wait_tile(1)
    bias_total = dscore_pass(0)
    products(0)
    bias_total = bias_total + dscore_pass(1)
    send_keys(0)
    wait_keys(2)
    wait_tile(2)
    score_pass(2)
    bias_total = bias_total + dscore_pass(2)
    zc_copies = spread(bias_total, 0, zc_peers, bias_zc, 2 * z + core, zc_ss, zc_rs)
    products(1)
    products(2)
    send_keys(1)
    send_keys(2)
    bias_total = gathered(bias_zc, zc_copies)
    xy_copies = spread(bias_total, 1, xy_peers, bias_xy, CHIPS * x + y, xy_ss, xy_rs)
    bias_out[...] = gathered(bias_xy, xy_copies)

    for c in kv_copies.values():
        c.wait_send()
    for c in sib_copies:
        c.wait_send()
    for c in fwd_copies.values():
        c.wait_send()
    for c in qa_copies.values():
        c.wait_send()
    for c in z_copies:
        c.wait_send()
    for c in own_copies + out_copies:
        c.wait()


def finish_kernel(
    half_rows,
    quart_rows,
    dq,
    dkv,
    bias,
    d_query,
    d_key,
    d_value,
    d_half_key,
    d_half_value,
    d_quart_key,
    d_quart_value,
    d_bias,
):
    heads = dq.shape[0]
    rows = d_key.shape[0]
    quart_at = dkv.shape[1] - 16
    for i in range(heads // 2):
        cols = slice(i * LANES, (i + 1) * LANES)
        d_query[:, cols] = dq[2 * i : 2 * i + 2].reshape(LANES, rows).T
        low, high = dkv[2 * i], dkv[2 * i + 1]
        swap_low, swap_high = 2 * i % HEADS == 1, (2 * i + 1) % HEADS == 1
        for value, outs in (
            (0, (d_key, d_half_key, d_quart_key)),
            (1, (d_value, d_half_value, d_quart_value)),
        ):
            both = joined(low, value ^ swap_low, high, value ^ swap_high)
            outs[0][:, cols] = both[:rows]
            outs[1][:, cols] = both[rows : rows + half_rows]
            outs[2][:, cols] = both[quart_at : quart_at + quart_rows]
    d_bias[...] = bias[: d_bias.shape[0], : d_bias.shape[1]]


def shards(
    cur_query,
    cur_key,
    cur_value,
    grad_out,
    out_weight,
    half_key,
    half_value,
    quart_key,
    quart_value,
    cur_count,
    section_bias,
    n_x,
    n_z,
):
    rows, width = cur_query.shape
    half_rows, quart_rows = half_key.shape[0], quart_key.shape[0]
    heads = width // HD
    block = rows + 48
    counts = cur_count.T
    hbm = pl.BlockSpec(memory_space=pltpu.HBM)
    vmem = pl.BlockSpec(memory_space=pltpu.VMEM)
    dma = pltpu.SemaphoreType.DMA
    queries = CHIPS * rows
    shards_n = 2 * CHIPS
    pair = [dma((HEADS, CHIPS)), dma((HEADS, CHIPS))]
    triple = [dma((HEADS,)), dma((HEADS,))]
    dq, dkv, bias = pl.pallas_call(
        functools.partial(exchange_kernel, n_x, n_z),
        out_shape=(
            jax.ShapeDtypeStruct((heads, HD, rows), BF),
            jax.ShapeDtypeStruct((heads, block, LANES), BF),
            jax.ShapeDtypeStruct((8, LANES), F32),
        ),
        in_specs=[hbm] * 11,
        out_specs=(hbm, hbm, vmem),
        scratch_shapes=[
            pltpu.VMEM((rows, width), BF),
            pltpu.VMEM((rows, width), BF),
            pltpu.VMEM((rows, width), BF),
            pltpu.VMEM((rows, width), BF),
            pltpu.VMEM((rows, width), BF),
            pltpu.VMEM(out_weight.shape, BF),
            pltpu.VMEM(half_key.shape, BF),
            pltpu.VMEM(half_value.shape, BF),
            pltpu.VMEM(quart_key.shape, BF),
            pltpu.VMEM(quart_value.shape, BF),
            pltpu.SMEM(counts.shape, jnp.int32),
            pltpu.SMEM(section_bias.shape, F32),
            pltpu.VMEM((heads, block, LANES), BF),
            pltpu.VMEM((heads, rows, LANES), BF),
            pltpu.VMEM((HEADS, 2, CHIPS, block, LANES), BF),
            pltpu.VMEM((HEADS, CHIPS, rows, LANES), BF),
            pltpu.VMEM((shards_n, rows, LANES), F32),
            pltpu.VMEM((HEADS, 8, queries), F32),
            pltpu.VMEM((HEADS, shards_n, block, queries), F32),
            pltpu.VMEM((shards_n, block, queries), F32),
            pltpu.VMEM((HEADS, shards_n * block, 2 * queries), BF),
            pltpu.VMEM((HEADS, CHIPS * block, LANES), BF),
            pltpu.VMEM((HEADS, CHIPS * block, LANES), BF),
            pltpu.VMEM((HEADS, CHIPS * block, LANES), F32),
            pltpu.VMEM((HEADS, CHIPS, block, LANES), BF),
            pltpu.VMEM((HEADS, CHIPS, HD, rows), BF),
            pltpu.VMEM((2, 8, LANES), F32),
            pltpu.VMEM((2 * n_z, 8, LANES), F32),
            pltpu.VMEM((n_x * CHIPS, 8, LANES), F32),
            dma((11,)),
            dma((FAR,)),
            dma((FAR,)),
            *pair,
            *triple,
            *pair,
            *pair,
            *triple,
            *pair,
            *pair,
            dma((2 * n_z,)),
            dma((2 * n_z,)),
            dma((n_x * CHIPS,)),
            dma((n_x * CHIPS,)),
        ],
        compiler_params=pltpu.CompilerParams(
            collective_id=0, has_side_effects=True, vmem_limit_bytes=62 << 20
        ),
        name="exchange",
    )(
        cur_query,
        cur_key,
        cur_value,
        grad_out,
        out_weight,
        half_key,
        half_value,
        quart_key,
        quart_value,
        counts,
        section_bias,
    )
    like = lambda a: jax.ShapeDtypeStruct(a.shape, a.dtype)
    return pl.pallas_call(
        functools.partial(finish_kernel, half_rows, quart_rows),
        out_shape=(
            like(cur_query),
            like(cur_key),
            like(cur_value),
            like(half_key),
            like(half_value),
            like(quart_key),
            like(quart_value),
            like(section_bias),
        ),
        in_specs=[vmem] * 3,
        out_specs=(vmem,) * 8,
        compiler_params=pltpu.CompilerParams(vmem_limit_bytes=62 << 20),
        name="finish",
    )(dq, dkv, bias)


def solution(mesh):
    n_z = 4
    n_x = mesh.shape["seq"] // (2 * CHIPS * n_z)
    return jax.shard_map(
        functools.partial(shards, n_x=n_x, n_z=n_z),
        mesh=mesh,
        in_specs=(
            P("seq", "head"),
            P("seq", "head"),
            P("seq", "head"),
            P("seq", "head"),
            P(None, "head"),
            P("seq", "head"),
            P("seq", "head"),
            P("seq", "head"),
            P("seq", "head"),
            P(),
            P(None, "head"),
        ),
        out_specs=(
            P("seq", "head"),
            P("seq", "head"),
            P("seq", "head"),
            P("seq", "head"),
            P("seq", "head"),
            P("seq", "head"),
            P("seq", "head"),
            P(None, "head"),
        ),
        check_vma=False,
    )
```

```python
import functools

import jax
import jax.numpy as jnp
from jax import lax
from jax.experimental import pallas as pl
from jax.experimental.pallas import tpu as pltpu
from jax.sharding import PartitionSpec as P

HD = 64
LANES = 128
CHIPS = 4
HEADS = 3
FAR = 3
MESH = pl.DeviceIdType.MESH
BF = jnp.bfloat16
F32 = jnp.float32


def dot(a, b, ca, cb):
    return lax.dot_general(a, b, (((ca,), (cb,)), ((), ())), preferred_element_type=F32)


def joined(a, head_a, b, head_b):
    return jnp.concatenate(
        [a[:, head_a * HD : (head_a + 1) * HD], b[:, head_b * HD : (head_b + 1) * HD]], axis=1
    )


def exchange_kernel(
    n_x,
    n_z,
    query_hbm,
    key_hbm,
    value_hbm,
    grad_hbm,
    weight_hbm,
    half_key_hbm,
    half_value_hbm,
    quart_key_hbm,
    quart_value_hbm,
    counts_hbm,
    section_bias_hbm,
    dq_out,
    dkv_out,
    bias_out,
    query,
    key,
    value,
    grad,
    grad_far,
    weight,
    half_key,
    half_value,
    quart_key,
    quart_value,
    counts,
    section_bias,
    kv_send,
    qa_send,
    kv_all,
    qa_all,
    count_bias,
    tops,
    scores,
    d_probs,
    low,
    part_send,
    part_got,
    own_sum,
    dkv_send,
    dq_send,
    bias_send,
    bias_zc,
    bias_xy,
    load_sem,
    z_ss,
    z_rs,
    kv_ss,
    kv_rs,
    sib_ss,
    sib_rs,
    fwd_ss,
    fwd_rs,
    qa_ss,
    qa_rs,
    part_ss,
    part_rs,
    dkv_ss,
    dkv_rs,
    dq_ss,
    dq_rs,
    zc_ss,
    zc_rs,
    xy_ss,
    xy_rs,
    round_sem,
):
    rows = query_hbm.shape[0]
    half_rows = half_key_hbm.shape[0]
    quart_rows = quart_key_hbm.shape[0]
    width = query_hbm.shape[1]
    block = kv_send.shape[1]
    quart_at = block - 16
    heads = width // HD
    seq = lax.axis_index("seq")
    head = lax.axis_index("head")
    core = seq % 2
    y = seq // 2 % CHIPS
    z = seq // 8 % n_z
    x = seq // (8 * n_z)
    clip = seq // 8

    def device(x, z, y, core):
        return ((x * n_z + z) * CHIPS + y) * 2 + core

    def chip(dy):
        return (y + dy) % CHIPS

    def copy(src, dst, ss, rs, seq_to, head_to=None):
        return pltpu.make_async_remote_copy(
            src_ref=src,
            dst_ref=dst,
            send_sem=ss,
            recv_sem=rs,
            device_id={"seq": seq_to, "head": head if head_to is None else head_to},
            device_id_type=MESH,
        )

    loads = [
        pltpu.make_async_copy(a, b, load_sem.at[i])
        for i, (a, b) in enumerate(
            [
                (query_hbm, query),
                (key_hbm, key),
                (value_hbm, value),
                (half_key_hbm, half_key),
                (half_value_hbm, half_value),
                (quart_key_hbm, quart_key),
                (quart_value_hbm, quart_value),
                (counts_hbm, counts),
                (section_bias_hbm, section_bias),
                (grad_hbm, grad),
                (weight_hbm, weight),
            ]
        )
    ]
    for load in loads:
        load.start()

    sibling = device(x, z, y, 1 - core)
    zc_peers = [
        device(x, (z + d) % n_z, y, (core + p) % 2) for d in range(n_z) for p in range(2)
    ][1:]
    xy_peers = [device((x + d) % n_x, z, chip(dy), core) for d in range(n_x) for dy in range(CHIPS)][1:]
    near_peers = [sibling] + [device(x, z, chip(dy), core) for dy in range(1, CHIPS)]
    near_peers += [device((x + d) % n_x, z, y, core) for d in (1, n_x - 1)]
    near_peers += [device(x, (z + d) % n_z, y, core) for d in (1, n_z - 1)]
    partners = [(seq, 1 - head)] + [(peer, head) for peer in near_peers]
    barrier = pltpu.get_barrier_semaphore()
    for seq_to, head_to in partners:
        pl.semaphore_signal(
            barrier, inc=1, device_id={"seq": seq_to, "head": head_to}, device_id_type=MESH
        )

    for load in loads[:7]:
        load.wait()
    zeros = jnp.zeros((block - rows, LANES), BF)
    for h in range(heads):
        first, second = (value, key) if h % HEADS == 1 else (key, value)
        kv_send[h, :rows] = joined(first, h, second, h)
        kv_send[h, rows:] = zeros
        first, second = (half_value, half_key) if h % HEADS == 1 else (half_key, half_value)
        kv_send[h, rows : rows + half_rows] = joined(first, h, second, h)
        first, second = (quart_value, quart_key) if h % HEADS == 1 else (quart_key, quart_value)
        kv_send[h, quart_at : quart_at + quart_rows] = joined(first, h, second, h)
    query[...] = query[...] * BF(HD**-0.5)
    for c in range(CHIPS):
        qa_send[HEADS * c] = joined(query, HEADS * c, query, HEADS * c + 1)

    pl.semaphore_wait(barrier, len(partners))

    far_cols = width // FAR
    z_copies = []
    for i in range(FAR):
        cols = slice(i * far_cols, (i + 1) * far_cols)
        c = copy(
            grad_hbm.at[:, cols], grad_far.at[:, cols], z_ss.at[i], z_rs.at[i], seq, 1 - head
        )
        c.start()
        z_copies.append(c)
    qa_copies = {}

    def greet(i):
        for peer in near_peers:
            pl.semaphore_signal(
                round_sem.at[i], inc=1, device_id={"seq": peer, "head": head}, device_id_type=MESH
            )

    def greeted(i):
        pl.semaphore_wait(round_sem.at[i], len(near_peers))

    def send_tile(t):
        for dy in (1, 3, 2):
            c = copy(
                qa_send.at[HEADS * chip(dy) + t],
                qa_all.at[t, dy],
                qa_ss.at[t, dy],
                qa_rs.at[t, dy],
                device(x, z, chip(dy), core),
            )
            c.start()
            qa_copies[t, dy] = c
        qa_all[t, 0] = qa_send[HEADS * y + t]

    send_tile(0)
    kv_copies = {}
    sib_copies = []
    for j in range(HEADS):
        for dy in (1, 3, 2):
            c = copy(
                kv_send.at[HEADS * chip(dy) + j],
                kv_all.at[j, 0, dy],
                kv_ss.at[j, dy],
                kv_rs.at[j, dy],
                device(x, z, chip(dy), core),
            )
            c.start()
            kv_copies[j, dy] = c
        c = copy(
            kv_send.at[HEADS * y + j], kv_all.at[j, 1, 0], sib_ss.at[j], sib_rs.at[j], sibling
        )
        c.start()
        sib_copies.append(c)
        kv_all[j, 0, 0] = kv_send[HEADS * y + j]

    greet(0)
    loads[7].wait()
    loads[8].wait()
    row_id = lax.broadcasted_iota(jnp.int32, (rows, LANES), 0)
    for c in range(2 * CHIPS):
        p, dy = divmod(c, CHIPS)
        shard = 2 * chip(CHIPS - dy) + (core if p == 0 else 1 - core)
        count_bias[c] = jnp.where(row_id < counts[shard, clip], F32(0), F32(-1e30))

    loads[9].wait()
    loads[10].wait()
    adjoint = dot(grad[...], weight[pl.ds(pl.multiple_of(head * width, LANES), width), :], 1, 0)

    fwd_copies = {}

    def forward(j):
        for dy in (1, 3, 2):
            kv_copies[j, dy].wait_recv()
            c = copy(
                kv_all.at[j, 0, dy],
                kv_all.at[j, 1, dy],
                fwd_ss.at[j, dy],
                fwd_rs.at[j, dy],
                sibling,
            )
            c.start()
            fwd_copies[j, dy] = c

    forward(0)
    for i in range(FAR):
        z_copies[i].wait_recv()
        at = pl.multiple_of((1 - head) * width + i * far_cols, LANES)
        adjoint += dot(
            grad_far[:, i * far_cols : (i + 1) * far_cols], weight[pl.ds(at, far_cols), :], 1, 0
        )
    own_count = counts[2 * y + core, clip]
    row_wide = lax.broadcasted_iota(jnp.int32, (rows, width), 0)
    adjoint = jnp.where(row_wide < own_count, adjoint, F32(0)).astype(BF)
    for c in range(CHIPS):
        qa_send[HEADS * c + 1] = joined(adjoint, HEADS * c + 1, adjoint, HEADS * c)
    send_tile(1)
    for c in range(CHIPS):
        qa_send[HEADS * c + 2] = joined(query, HEADS * c + 2, adjoint, HEADS * c + 2)
    send_tile(2)

    bias_row = lax.broadcasted_iota(jnp.int32, (8, LANES), 0)
    bias_lane = lax.broadcasted_iota(jnp.int32, (8, LANES), 1)
    hist_id = lax.broadcasted_iota(jnp.int32, (block - rows, LANES), 0)
    queries = CHIPS * rows
    groups = queries // LANES
    low_lane = lax.broadcasted_iota(jnp.int32, (queries, LANES), 1) < HD

    def fold(t, op):
        total = t[:8]
        for r in range(8, t.shape[0], 8):
            total = op(total, t[r : r + 8])
        return total

    def wait_tile(t):
        for dy in (1, 3, 2):
            qa_copies[t, dy].wait_recv()

    def wait_keys(j):
        for dy in (1, 3, 2):
            fwd_copies[j, dy].wait_recv()
        sib_copies[j].wait_recv()

    def query_part(j):
        tile = qa_all[2 if j == 2 else 0].reshape(queries, LANES)
        return jnp.where(low_lane, BF(0), tile) if j == 1 else jnp.where(low_lane, tile, BF(0))

    def adjoint_part(j):
        tile = qa_all[2 if j == 2 else 1].reshape(queries, LANES)
        return jnp.where(low_lane, tile, BF(0)) if j == 1 else jnp.where(low_lane, BF(0), tile)

    def score_pass(j):
        my_head = HEADS * y + j
        half_bias = section_bias[0, my_head]
        quart_bias = section_bias[1, my_head]
        hist_bias = jnp.where(
            hist_id < half_rows,
            half_bias,
            jnp.where(
                (hist_id >= quart_at - rows) & (hist_id < quart_at - rows + quart_rows),
                quart_bias,
                F32(-1e30),
            ),
        )
        q_part = query_part(j)
        top = jnp.full((8, queries), -3e38, F32)
        for c in range(2 * CHIPS):
            s = dot(kv_all[j, c // CHIPS, c % CHIPS], q_part, 1, 1)
            bias = jnp.concatenate([count_bias[c], hist_bias], axis=0)
            s = s + jnp.concatenate([bias] * groups, axis=1)
            scores[j, c] = s
            top = jnp.maximum(top, fold(s, jnp.maximum))
        tops[j] = top

    def dscore_pass(j):
        a_part = adjoint_part(j)
        top = jnp.max(tops[j], axis=0, keepdims=True)
        total = jnp.zeros((8, queries), F32)
        delta = jnp.zeros((8, queries), F32)
        for c in range(2 * CHIPS):
            dp = dot(kv_all[j, c // CHIPS, c % CHIPS], a_part, 1, 1)
            e = jnp.exp(scores[j, c] - top)
            scores[j, c] = e
            d_probs[c] = dp
            total = total + fold(e, jnp.add)
            delta = delta + fold(e * dp, jnp.add)
        inverse = 1.0 / jnp.sum(total, axis=0, keepdims=True)
        delta = jnp.sum(delta, axis=0, keepdims=True) * inverse
        half_sum = jnp.zeros((8, queries), F32)
        quart_sum = jnp.zeros((8, queries), F32)
        for c in range(2 * CHIPS):
            probs = scores[j, c] * inverse
            ds = probs * (d_probs[c] - delta)
            half_sum = half_sum + fold(ds[rows:quart_at], jnp.add)
            quart_sum = quart_sum + fold(ds[quart_at:], jnp.add)
            low[j, c * block : (c + 1) * block, :queries] = ds.astype(BF)
            low[j, c * block : (c + 1) * block, queries:] = probs.astype(BF)
        return jnp.where(
            bias_lane == HEADS * y + j,
            jnp.where(bias_row == 0, jnp.sum(half_sum), jnp.sum(quart_sum)),
            F32(0),
        )

    part_copies = {}
    out_copies = []
    own_copies = []

    def products(j):
        my_head = HEADS * y + j
        near = CHIPS * block
        both = jnp.concatenate([query_part(j), adjoint_part(j)], axis=0)
        kv = kv_all[j].reshape(2 * near, LANES)
        at = HD if j == 1 else 0
        dq = (dot(kv, low[j, :, :queries], 0, 0)[at : at + HD] * F32(HD**-0.5)).astype(BF)
        for dy in range(CHIPS):
            dq_send[j, dy] = dq[:, dy * rows : (dy + 1) * rows]
        for dy in (1, 3, 2):
            c = copy(
                dq_send.at[j, dy],
                dq_out.at[my_head],
                dq_ss.at[j, dy],
                dq_rs.at[j, dy],
                device(x, z, chip(CHIPS - dy), core),
            )
            c.start()
            out_copies.append(c)
        c = pltpu.make_async_copy(dq_send.at[j, 0], dq_out.at[my_head], dq_ss.at[j, 0])
        c.start()
        own_copies.append(c)
        grads = dot(both, low[j], 0, 1).T
        part_send[j] = grads[near:].astype(BF)
        c = copy(part_send.at[j], part_got.at[j], part_ss.at[j], part_rs.at[j], sibling)
        c.start()
        part_copies[j] = c
        own_sum[j] = grads[:near]

    def send_keys(j):
        my_head = HEADS * y + j
        part_copies[j].wait()
        for dy in (1, 3, 2, 0):
            at = slice(dy * block, (dy + 1) * block)
            dkv_send[j, dy] = (own_sum[j, at] + part_got[j, at].astype(F32)).astype(BF)
            if dy == 0:
                c = pltpu.make_async_copy(dkv_send.at[j, 0], dkv_out.at[my_head], dkv_ss.at[j, 0])
                c.start()
                own_copies.append(c)
                continue
            c = copy(
                dkv_send.at[j, dy],
                dkv_out.at[my_head],
                dkv_ss.at[j, dy],
                dkv_rs.at[j, dy],
                device(x, z, chip(CHIPS - dy), core),
            )
            c.start()
            out_copies.append(c)

    def spread(total, stage, peers, slots, me, ss, rs):
        bias_send[stage] = total
        slots[me] = total
        copies = []
        for i, peer in enumerate(peers):
            c = copy(bias_send.at[stage], slots.at[me], ss.at[i], rs.at[i], peer)
            c.start()
            copies.append(c)
        return copies

    def gathered(slots, copies):
        for c in copies:
            c.wait()
        total = slots[0]
        for i in range(1, len(copies) + 1):
            total = total + slots[i]
        return total

    greeted(0)
    greet(1)
    wait_tile(0)
    wait_keys(0)
    score_pass(0)
    forward(1)
    wait_keys(1)
    score_pass(1)
    forward(2)
    wait_tile(1)
    bias_total = dscore_pass(0)
    products(0)
    bias_total = bias_total + dscore_pass(1)
    send_keys(0)
    wait_keys(2)
    wait_tile(2)
    score_pass(2)
    bias_total = bias_total + dscore_pass(2)
    greeted(1)
    zc_copies = spread(bias_total, 0, zc_peers, bias_zc, 2 * z + core, zc_ss, zc_rs)
    products(1)
    products(2)
    send_keys(1)
    send_keys(2)
    bias_total = gathered(bias_zc, zc_copies)
    xy_copies = spread(bias_total, 1, xy_peers, bias_xy, CHIPS * x + y, xy_ss, xy_rs)
    bias_out[...] = gathered(bias_xy, xy_copies)

    for c in kv_copies.values():
        c.wait_send()
    for c in sib_copies:
        c.wait_send()
    for c in fwd_copies.values():
        c.wait_send()
    for c in qa_copies.values():
        c.wait_send()
    for c in z_copies:
        c.wait_send()
    for c in own_copies + out_copies:
        c.wait()


def finish_kernel(
    half_rows,
    quart_rows,
    dq,
    dkv,
    bias,
    d_query,
    d_key,
    d_value,
    d_half_key,
    d_half_value,
    d_quart_key,
    d_quart_value,
    d_bias,
):
    heads = dq.shape[0]
    rows = d_key.shape[0]
    quart_at = dkv.shape[1] - 16
    for i in range(heads // 2):
        cols = slice(i * LANES, (i + 1) * LANES)
        d_query[:, cols] = dq[2 * i : 2 * i + 2].reshape(LANES, rows).T
        low, high = dkv[2 * i], dkv[2 * i + 1]
        swap_low, swap_high = 2 * i % HEADS == 1, (2 * i + 1) % HEADS == 1
        for value, outs in (
            (0, (d_key, d_half_key, d_quart_key)),
            (1, (d_value, d_half_value, d_quart_value)),
        ):
            both = joined(low, value ^ swap_low, high, value ^ swap_high)
            outs[0][:, cols] = both[:rows]
            outs[1][:, cols] = both[rows : rows + half_rows]
            outs[2][:, cols] = both[quart_at : quart_at + quart_rows]
    d_bias[...] = bias[: d_bias.shape[0], : d_bias.shape[1]]


def shards(
    cur_query,
    cur_key,
    cur_value,
    grad_out,
    out_weight,
    half_key,
    half_value,
    quart_key,
    quart_value,
    cur_count,
    section_bias,
    n_x,
    n_z,
):
    rows, width = cur_query.shape
    half_rows, quart_rows = half_key.shape[0], quart_key.shape[0]
    heads = width // HD
    block = rows + 48
    counts = cur_count.T
    hbm = pl.BlockSpec(memory_space=pltpu.HBM)
    vmem = pl.BlockSpec(memory_space=pltpu.VMEM)
    dma = pltpu.SemaphoreType.DMA
    queries = CHIPS * rows
    shards_n = 2 * CHIPS
    pair = [dma((HEADS, CHIPS)), dma((HEADS, CHIPS))]
    triple = [dma((HEADS,)), dma((HEADS,))]
    dq, dkv, bias = pl.pallas_call(
        functools.partial(exchange_kernel, n_x, n_z),
        out_shape=(
            jax.ShapeDtypeStruct((heads, HD, rows), BF),
            jax.ShapeDtypeStruct((heads, block, LANES), BF),
            jax.ShapeDtypeStruct((8, LANES), F32),
        ),
        in_specs=[hbm] * 11,
        out_specs=(hbm, hbm, vmem),
        scratch_shapes=[
            pltpu.VMEM((rows, width), BF),
            pltpu.VMEM((rows, width), BF),
            pltpu.VMEM((rows, width), BF),
            pltpu.VMEM((rows, width), BF),
            pltpu.VMEM((rows, width), BF),
            pltpu.VMEM(out_weight.shape, BF),
            pltpu.VMEM(half_key.shape, BF),
            pltpu.VMEM(half_value.shape, BF),
            pltpu.VMEM(quart_key.shape, BF),
            pltpu.VMEM(quart_value.shape, BF),
            pltpu.SMEM(counts.shape, jnp.int32),
            pltpu.SMEM(section_bias.shape, F32),
            pltpu.VMEM((heads, block, LANES), BF),
            pltpu.VMEM((heads, rows, LANES), BF),
            pltpu.VMEM((HEADS, 2, CHIPS, block, LANES), BF),
            pltpu.VMEM((HEADS, CHIPS, rows, LANES), BF),
            pltpu.VMEM((shards_n, rows, LANES), F32),
            pltpu.VMEM((HEADS, 8, queries), F32),
            pltpu.VMEM((HEADS, shards_n, block, queries), F32),
            pltpu.VMEM((shards_n, block, queries), F32),
            pltpu.VMEM((HEADS, shards_n * block, 2 * queries), BF),
            pltpu.VMEM((HEADS, CHIPS * block, LANES), BF),
            pltpu.VMEM((HEADS, CHIPS * block, LANES), BF),
            pltpu.VMEM((HEADS, CHIPS * block, LANES), F32),
            pltpu.VMEM((HEADS, CHIPS, block, LANES), BF),
            pltpu.VMEM((HEADS, CHIPS, HD, rows), BF),
            pltpu.VMEM((2, 8, LANES), F32),
            pltpu.VMEM((2 * n_z, 8, LANES), F32),
            pltpu.VMEM((n_x * CHIPS, 8, LANES), F32),
            dma((11,)),
            dma((FAR,)),
            dma((FAR,)),
            *pair,
            *triple,
            *pair,
            *pair,
            *triple,
            *pair,
            *pair,
            dma((2 * n_z,)),
            dma((2 * n_z,)),
            dma((n_x * CHIPS,)),
            dma((n_x * CHIPS,)),
            pltpu.SemaphoreType.REGULAR((2,)),
        ],
        compiler_params=pltpu.CompilerParams(
            collective_id=0, has_side_effects=True, vmem_limit_bytes=62 << 20
        ),
        name="exchange",
    )(
        cur_query,
        cur_key,
        cur_value,
        grad_out,
        out_weight,
        half_key,
        half_value,
        quart_key,
        quart_value,
        counts,
        section_bias,
    )
    like = lambda a: jax.ShapeDtypeStruct(a.shape, a.dtype)
    return pl.pallas_call(
        functools.partial(finish_kernel, half_rows, quart_rows),
        out_shape=(
            like(cur_query),
            like(cur_key),
            like(cur_value),
            like(half_key),
            like(half_value),
            like(quart_key),
            like(quart_value),
            like(section_bias),
        ),
        in_specs=[vmem] * 3,
        out_specs=(vmem,) * 8,
        compiler_params=pltpu.CompilerParams(vmem_limit_bytes=62 << 20),
        name="finish",
    )(dq, dkv, bias)


def solution(mesh):
    n_z = 4
    n_x = mesh.shape["seq"] // (2 * CHIPS * n_z)
    return jax.shard_map(
        functools.partial(shards, n_x=n_x, n_z=n_z),
        mesh=mesh,
        in_specs=(
            P("seq", "head"),
            P("seq", "head"),
            P("seq", "head"),
            P("seq", "head"),
            P(None, "head"),
            P("seq", "head"),
            P("seq", "head"),
            P("seq", "head"),
            P("seq", "head"),
            P(),
            P(None, "head"),
        ),
        out_specs=(
            P("seq", "head"),
            P("seq", "head"),
            P("seq", "head"),
            P("seq", "head"),
            P("seq", "head"),
            P("seq", "head"),
            P("seq", "head"),
            P(None, "head"),
        ),
        check_vma=False,
    )
```

```python
import functools

import jax
import jax.numpy as jnp
from jax import lax
from jax.experimental import pallas as pl
from jax.experimental.pallas import tpu as pltpu
from jax.sharding import PartitionSpec as P

HD = 64
LANES = 128
CHIPS = 4
HEADS = 3
FAR = 3
MESH = pl.DeviceIdType.MESH
BF = jnp.bfloat16
F32 = jnp.float32


def dot(a, b, ca, cb):
    return lax.dot_general(a, b, (((ca,), (cb,)), ((), ())), preferred_element_type=F32)


def joined(a, head_a, b, head_b):
    return jnp.concatenate(
        [a[:, head_a * HD : (head_a + 1) * HD], b[:, head_b * HD : (head_b + 1) * HD]], axis=1
    )


def exchange_kernel(
    n_x,
    n_z,
    query_hbm,
    key_hbm,
    value_hbm,
    grad_hbm,
    weight_hbm,
    half_key_hbm,
    half_value_hbm,
    quart_key_hbm,
    quart_value_hbm,
    counts_hbm,
    section_bias_hbm,
    dq_out,
    dkv_out,
    bias_out,
    query,
    key,
    value,
    grad,
    grad_far,
    weight,
    half_key,
    half_value,
    quart_key,
    quart_value,
    counts,
    section_bias,
    kv_send,
    qa_send,
    kv_all,
    qa_all,
    count_bias,
    tops,
    scores,
    d_probs,
    low,
    part_send,
    part_got,
    own_sum,
    dkv_send,
    dq_send,
    bias_send,
    bias_zc,
    bias_xy,
    load_sem,
    z_ss,
    z_rs,
    kv_ss,
    kv_rs,
    sib_ss,
    sib_rs,
    fwd_ss,
    fwd_rs,
    qa_ss,
    qa_rs,
    part_ss,
    part_rs,
    dkv_ss,
    dkv_rs,
    dq_ss,
    dq_rs,
    zc_ss,
    zc_rs,
    xy_ss,
    xy_rs,
    round_sem,
):
    rows = query_hbm.shape[0]
    half_rows = half_key_hbm.shape[0]
    quart_rows = quart_key_hbm.shape[0]
    width = query_hbm.shape[1]
    block = kv_send.shape[1]
    quart_at = block - 16
    heads = width // HD
    seq = lax.axis_index("seq")
    head = lax.axis_index("head")
    core = seq % 2
    y = seq // 2 % CHIPS
    z = seq // 8 % n_z
    x = seq // (8 * n_z)
    clip = seq // 8

    def device(x, z, y, core):
        return ((x * n_z + z) * CHIPS + y) * 2 + core

    def chip(dy):
        return (y + dy) % CHIPS

    def copy(src, dst, ss, rs, seq_to, head_to=None):
        return pltpu.make_async_remote_copy(
            src_ref=src,
            dst_ref=dst,
            send_sem=ss,
            recv_sem=rs,
            device_id={"seq": seq_to, "head": head if head_to is None else head_to},
            device_id_type=MESH,
        )

    loads = [
        pltpu.make_async_copy(a, b, load_sem.at[i])
        for i, (a, b) in enumerate(
            [
                (query_hbm, query),
                (key_hbm, key),
                (value_hbm, value),
                (half_key_hbm, half_key),
                (half_value_hbm, half_value),
                (quart_key_hbm, quart_key),
                (quart_value_hbm, quart_value),
                (counts_hbm, counts),
                (section_bias_hbm, section_bias),
                (grad_hbm, grad),
                (weight_hbm, weight),
            ]
        )
    ]
    for load in loads:
        load.start()

    sibling = device(x, z, y, 1 - core)
    zc_peers = [
        device(x, (z + d) % n_z, y, (core + p) % 2) for d in range(n_z) for p in range(2)
    ][1:]
    xy_peers = [device((x + d) % n_x, z, chip(dy), core) for d in range(n_x) for dy in range(CHIPS)][1:]
    near_peers = [sibling] + [device(x, z, chip(dy), core) for dy in range(1, CHIPS)]
    near_peers += [device((x + d) % n_x, z, y, core) for d in (1, n_x - 1)]
    near_peers += [device(x, (z + d) % n_z, y, core) for d in (1, n_z - 1)]
    partners = [(seq, 1 - head)] + [(peer, head) for peer in near_peers]
    barrier = pltpu.get_barrier_semaphore()
    for seq_to, head_to in partners:
        pl.semaphore_signal(
            barrier, inc=1, device_id={"seq": seq_to, "head": head_to}, device_id_type=MESH
        )

    for load in loads[:7]:
        load.wait()
    zeros = jnp.zeros((block - rows, LANES), BF)
    for h in range(heads):
        first, second = (value, key) if h % HEADS == 1 else (key, value)
        kv_send[h, :rows] = joined(first, h, second, h)
        kv_send[h, rows:] = zeros
        first, second = (half_value, half_key) if h % HEADS == 1 else (half_key, half_value)
        kv_send[h, rows : rows + half_rows] = joined(first, h, second, h)
        first, second = (quart_value, quart_key) if h % HEADS == 1 else (quart_key, quart_value)
        kv_send[h, quart_at : quart_at + quart_rows] = joined(first, h, second, h)
    query[...] = query[...] * BF(HD**-0.5)
    for c in range(CHIPS):
        qa_send[HEADS * c] = joined(query, HEADS * c, query, HEADS * c + 1)

    pl.semaphore_wait(barrier, len(partners))

    far_cols = width // FAR
    z_copies = []
    for i in range(FAR):
        cols = slice(i * far_cols, (i + 1) * far_cols)
        c = copy(
            grad_hbm.at[:, cols], grad_far.at[:, cols], z_ss.at[i], z_rs.at[i], seq, 1 - head
        )
        c.start()
        z_copies.append(c)
    qa_copies = {}

    def greet(i):
        for peer in near_peers:
            pl.semaphore_signal(
                round_sem.at[i], inc=1, device_id={"seq": peer, "head": head}, device_id_type=MESH
            )

    def greeted(i):
        pl.semaphore_wait(round_sem.at[i], len(near_peers))

    def send_tile(t):
        for dy in (2, 1, 3):
            c = copy(
                qa_send.at[HEADS * chip(dy) + t],
                qa_all.at[t, dy],
                qa_ss.at[t, dy],
                qa_rs.at[t, dy],
                device(x, z, chip(dy), core),
            )
            c.start()
            qa_copies[t, dy] = c
        qa_all[t, 0] = qa_send[HEADS * y + t]

    send_tile(0)
    kv_copies = {}
    sib_copies = []
    for j in range(HEADS):
        for dy in (2, 1, 3):
            c = copy(
                kv_send.at[HEADS * chip(dy) + j],
                kv_all.at[j, 0, dy],
                kv_ss.at[j, dy],
                kv_rs.at[j, dy],
                device(x, z, chip(dy), core),
            )
            c.start()
            kv_copies[j, dy] = c
        c = copy(
            kv_send.at[HEADS * y + j], kv_all.at[j, 1, 0], sib_ss.at[j], sib_rs.at[j], sibling
        )
        c.start()
        sib_copies.append(c)
        kv_all[j, 0, 0] = kv_send[HEADS * y + j]

    greet(0)
    loads[7].wait()
    loads[8].wait()
    row_id = lax.broadcasted_iota(jnp.int32, (rows, LANES), 0)
    for c in range(2 * CHIPS):
        p, dy = divmod(c, CHIPS)
        shard = 2 * chip(CHIPS - dy) + (core if p == 0 else 1 - core)
        count_bias[c] = jnp.where(row_id < counts[shard, clip], F32(0), F32(-1e30))

    loads[9].wait()
    loads[10].wait()
    adjoint = dot(grad[...], weight[pl.ds(pl.multiple_of(head * width, LANES), width), :], 1, 0)

    fwd_copies = {}

    def forward(j):
        for dy in (2, 1, 3):
            kv_copies[j, dy].wait_recv()
            c = copy(
                kv_all.at[j, 0, dy],
                kv_all.at[j, 1, dy],
                fwd_ss.at[j, dy],
                fwd_rs.at[j, dy],
                sibling,
            )
            c.start()
            fwd_copies[j, dy] = c

    forward(0)
    for i in range(FAR):
        z_copies[i].wait_recv()
        at = pl.multiple_of((1 - head) * width + i * far_cols, LANES)
        adjoint += dot(
            grad_far[:, i * far_cols : (i + 1) * far_cols], weight[pl.ds(at, far_cols), :], 1, 0
        )
    own_count = counts[2 * y + core, clip]
    row_wide = lax.broadcasted_iota(jnp.int32, (rows, width), 0)
    adjoint = jnp.where(row_wide < own_count, adjoint, F32(0)).astype(BF)
    for c in range(CHIPS):
        qa_send[HEADS * c + 1] = joined(adjoint, HEADS * c + 1, adjoint, HEADS * c)
    send_tile(1)
    for c in range(CHIPS):
        qa_send[HEADS * c + 2] = joined(query, HEADS * c + 2, adjoint, HEADS * c + 2)
    send_tile(2)

    bias_row = lax.broadcasted_iota(jnp.int32, (8, LANES), 0)
    bias_lane = lax.broadcasted_iota(jnp.int32, (8, LANES), 1)
    hist_id = lax.broadcasted_iota(jnp.int32, (block - rows, LANES), 0)
    queries = CHIPS * rows
    groups = queries // LANES
    low_lane = lax.broadcasted_iota(jnp.int32, (queries, LANES), 1) < HD

    def fold(t, op):
        total = t[:8]
        for r in range(8, t.shape[0], 8):
            total = op(total, t[r : r + 8])
        return total

    def wait_tile(t):
        for dy in (2, 1, 3):
            qa_copies[t, dy].wait_recv()

    def wait_keys(j):
        for dy in (2, 1, 3):
            fwd_copies[j, dy].wait_recv()
        sib_copies[j].wait_recv()

    def query_part(j):
        tile = qa_all[2 if j == 2 else 0].reshape(queries, LANES)
        return jnp.where(low_lane, BF(0), tile) if j == 1 else jnp.where(low_lane, tile, BF(0))

    def adjoint_part(j):
        tile = qa_all[2 if j == 2 else 1].reshape(queries, LANES)
        return jnp.where(low_lane, tile, BF(0)) if j == 1 else jnp.where(low_lane, BF(0), tile)

    def score_pass(j):
        my_head = HEADS * y + j
        half_bias = section_bias[0, my_head]
        quart_bias = section_bias[1, my_head]
        hist_bias = jnp.where(
            hist_id < half_rows,
            half_bias,
            jnp.where(
                (hist_id >= quart_at - rows) & (hist_id < quart_at - rows + quart_rows),
                quart_bias,
                F32(-1e30),
            ),
        )
        q_part = query_part(j)
        top = jnp.full((8, queries), -3e38, F32)
        for c in range(2 * CHIPS):
            s = dot(kv_all[j, c // CHIPS, c % CHIPS], q_part, 1, 1)
            bias = jnp.concatenate([count_bias[c], hist_bias], axis=0)
            s = s + jnp.concatenate([bias] * groups, axis=1)
            scores[j, c] = s
            top = jnp.maximum(top, fold(s, jnp.maximum))
        tops[j] = top

    def dscore_pass(j):
        a_part = adjoint_part(j)
        top = jnp.max(tops[j], axis=0, keepdims=True)
        total = jnp.zeros((8, queries), F32)
        delta = jnp.zeros((8, queries), F32)
        for c in range(2 * CHIPS):
            dp = dot(kv_all[j, c // CHIPS, c % CHIPS], a_part, 1, 1)
            e = jnp.exp(scores[j, c] - top)
            scores[j, c] = e
            d_probs[c] = dp
            total = total + fold(e, jnp.add)
            delta = delta + fold(e * dp, jnp.add)
        inverse = 1.0 / jnp.sum(total, axis=0, keepdims=True)
        delta = jnp.sum(delta, axis=0, keepdims=True) * inverse
        half_sum = jnp.zeros((8, queries), F32)
        quart_sum = jnp.zeros((8, queries), F32)
        for c in range(2 * CHIPS):
            probs = scores[j, c] * inverse
            ds = probs * (d_probs[c] - delta)
            half_sum = half_sum + fold(ds[rows:quart_at], jnp.add)
            quart_sum = quart_sum + fold(ds[quart_at:], jnp.add)
            low[j, c * block : (c + 1) * block, :queries] = ds.astype(BF)
            low[j, c * block : (c + 1) * block, queries:] = probs.astype(BF)
        return jnp.where(
            bias_lane == HEADS * y + j,
            jnp.where(bias_row == 0, jnp.sum(half_sum), jnp.sum(quart_sum)),
            F32(0),
        )

    part_copies = {}
    out_copies = []
    own_copies = []

    def products(j):
        my_head = HEADS * y + j
        near = CHIPS * block
        both = jnp.concatenate([query_part(j), adjoint_part(j)], axis=0)
        kv = kv_all[j].reshape(2 * near, LANES)
        at = HD if j == 1 else 0
        dq = (dot(kv, low[j, :, :queries], 0, 0)[at : at + HD] * F32(HD**-0.5)).astype(BF)
        for dy in range(CHIPS):
            dq_send[j, dy] = dq[:, dy * rows : (dy + 1) * rows]
        for dy in (2, 1, 3):
            c = copy(
                dq_send.at[j, dy],
                dq_out.at[my_head],
                dq_ss.at[j, dy],
                dq_rs.at[j, dy],
                device(x, z, chip(CHIPS - dy), core),
            )
            c.start()
            out_copies.append(c)
        c = pltpu.make_async_copy(dq_send.at[j, 0], dq_out.at[my_head], dq_ss.at[j, 0])
        c.start()
        own_copies.append(c)
        grads = dot(both, low[j], 0, 1).T
        part_send[j] = grads[near:].astype(BF)
        c = copy(part_send.at[j], part_got.at[j], part_ss.at[j], part_rs.at[j], sibling)
        c.start()
        part_copies[j] = c
        own_sum[j] = grads[:near]

    def send_keys(j):
        my_head = HEADS * y + j
        part_copies[j].wait()
        for dy in (2, 1, 3, 0):
            at = slice(dy * block, (dy + 1) * block)
            dkv_send[j, dy] = (own_sum[j, at] + part_got[j, at].astype(F32)).astype(BF)
            if dy == 0:
                c = pltpu.make_async_copy(dkv_send.at[j, 0], dkv_out.at[my_head], dkv_ss.at[j, 0])
                c.start()
                own_copies.append(c)
                continue
            c = copy(
                dkv_send.at[j, dy],
                dkv_out.at[my_head],
                dkv_ss.at[j, dy],
                dkv_rs.at[j, dy],
                device(x, z, chip(CHIPS - dy), core),
            )
            c.start()
            out_copies.append(c)

    def spread(total, stage, peers, slots, me, ss, rs):
        bias_send[stage] = total
        slots[me] = total
        copies = []
        for i, peer in enumerate(peers):
            c = copy(bias_send.at[stage], slots.at[me], ss.at[i], rs.at[i], peer)
            c.start()
            copies.append(c)
        return copies

    def gathered(slots, copies):
        for c in copies:
            c.wait()
        total = slots[0]
        for i in range(1, len(copies) + 1):
            total = total + slots[i]
        return total

    greeted(0)
    greet(1)
    wait_tile(0)
    wait_keys(0)
    score_pass(0)
    forward(1)
    wait_keys(1)
    score_pass(1)
    forward(2)
    wait_tile(1)
    bias_total = dscore_pass(0)
    products(0)
    bias_total = bias_total + dscore_pass(1)
    send_keys(0)
    wait_keys(2)
    wait_tile(2)
    score_pass(2)
    bias_total = bias_total + dscore_pass(2)
    greeted(1)
    zc_copies = spread(bias_total, 0, zc_peers, bias_zc, 2 * z + core, zc_ss, zc_rs)
    products(1)
    products(2)
    send_keys(1)
    send_keys(2)
    bias_total = gathered(bias_zc, zc_copies)
    xy_copies = spread(bias_total, 1, xy_peers, bias_xy, CHIPS * x + y, xy_ss, xy_rs)
    bias_out[...] = gathered(bias_xy, xy_copies)

    for c in kv_copies.values():
        c.wait_send()
    for c in sib_copies:
        c.wait_send()
    for c in fwd_copies.values():
        c.wait_send()
    for c in qa_copies.values():
        c.wait_send()
    for c in z_copies:
        c.wait_send()
    for c in own_copies + out_copies:
        c.wait()


def finish_kernel(
    half_rows,
    quart_rows,
    dq,
    dkv,
    bias,
    d_query,
    d_key,
    d_value,
    d_half_key,
    d_half_value,
    d_quart_key,
    d_quart_value,
    d_bias,
):
    heads = dq.shape[0]
    rows = d_key.shape[0]
    quart_at = dkv.shape[1] - 16
    for i in range(heads // 2):
        cols = slice(i * LANES, (i + 1) * LANES)
        d_query[:, cols] = dq[2 * i : 2 * i + 2].reshape(LANES, rows).T
        low, high = dkv[2 * i], dkv[2 * i + 1]
        swap_low, swap_high = 2 * i % HEADS == 1, (2 * i + 1) % HEADS == 1
        for value, outs in (
            (0, (d_key, d_half_key, d_quart_key)),
            (1, (d_value, d_half_value, d_quart_value)),
        ):
            both = joined(low, value ^ swap_low, high, value ^ swap_high)
            outs[0][:, cols] = both[:rows]
            outs[1][:, cols] = both[rows : rows + half_rows]
            outs[2][:, cols] = both[quart_at : quart_at + quart_rows]
    d_bias[...] = bias[: d_bias.shape[0], : d_bias.shape[1]]


def shards(
    cur_query,
    cur_key,
    cur_value,
    grad_out,
    out_weight,
    half_key,
    half_value,
    quart_key,
    quart_value,
    cur_count,
    section_bias,
    n_x,
    n_z,
):
    rows, width = cur_query.shape
    half_rows, quart_rows = half_key.shape[0], quart_key.shape[0]
    heads = width // HD
    block = rows + 48
    counts = cur_count.T
    hbm = pl.BlockSpec(memory_space=pltpu.HBM)
    vmem = pl.BlockSpec(memory_space=pltpu.VMEM)
    dma = pltpu.SemaphoreType.DMA
    queries = CHIPS * rows
    shards_n = 2 * CHIPS
    pair = [dma((HEADS, CHIPS)), dma((HEADS, CHIPS))]
    triple = [dma((HEADS,)), dma((HEADS,))]
    dq, dkv, bias = pl.pallas_call(
        functools.partial(exchange_kernel, n_x, n_z),
        out_shape=(
            jax.ShapeDtypeStruct((heads, HD, rows), BF),
            jax.ShapeDtypeStruct((heads, block, LANES), BF),
            jax.ShapeDtypeStruct((8, LANES), F32),
        ),
        in_specs=[hbm] * 11,
        out_specs=(hbm, hbm, vmem),
        scratch_shapes=[
            pltpu.VMEM((rows, width), BF),
            pltpu.VMEM((rows, width), BF),
            pltpu.VMEM((rows, width), BF),
            pltpu.VMEM((rows, width), BF),
            pltpu.VMEM((rows, width), BF),
            pltpu.VMEM(out_weight.shape, BF),
            pltpu.VMEM(half_key.shape, BF),
            pltpu.VMEM(half_value.shape, BF),
            pltpu.VMEM(quart_key.shape, BF),
            pltpu.VMEM(quart_value.shape, BF),
            pltpu.SMEM(counts.shape, jnp.int32),
            pltpu.SMEM(section_bias.shape, F32),
            pltpu.VMEM((heads, block, LANES), BF),
            pltpu.VMEM((heads, rows, LANES), BF),
            pltpu.VMEM((HEADS, 2, CHIPS, block, LANES), BF),
            pltpu.VMEM((HEADS, CHIPS, rows, LANES), BF),
            pltpu.VMEM((shards_n, rows, LANES), F32),
            pltpu.VMEM((HEADS, 8, queries), F32),
            pltpu.VMEM((HEADS, shards_n, block, queries), F32),
            pltpu.VMEM((shards_n, block, queries), F32),
            pltpu.VMEM((HEADS, shards_n * block, 2 * queries), BF),
            pltpu.VMEM((HEADS, CHIPS * block, LANES), BF),
            pltpu.VMEM((HEADS, CHIPS * block, LANES), BF),
            pltpu.VMEM((HEADS, CHIPS * block, LANES), F32),
            pltpu.VMEM((HEADS, CHIPS, block, LANES), BF),
            pltpu.VMEM((HEADS, CHIPS, HD, rows), BF),
            pltpu.VMEM((2, 8, LANES), F32),
            pltpu.VMEM((2 * n_z, 8, LANES), F32),
            pltpu.VMEM((n_x * CHIPS, 8, LANES), F32),
            dma((11,)),
            dma((FAR,)),
            dma((FAR,)),
            *pair,
            *triple,
            *pair,
            *pair,
            *triple,
            *pair,
            *pair,
            dma((2 * n_z,)),
            dma((2 * n_z,)),
            dma((n_x * CHIPS,)),
            dma((n_x * CHIPS,)),
            pltpu.SemaphoreType.REGULAR((2,)),
        ],
        compiler_params=pltpu.CompilerParams(
            collective_id=0, has_side_effects=True, vmem_limit_bytes=62 << 20
        ),
        name="exchange",
    )(
        cur_query,
        cur_key,
        cur_value,
        grad_out,
        out_weight,
        half_key,
        half_value,
        quart_key,
        quart_value,
        counts,
        section_bias,
    )
    like = lambda a: jax.ShapeDtypeStruct(a.shape, a.dtype)
    return pl.pallas_call(
        functools.partial(finish_kernel, half_rows, quart_rows),
        out_shape=(
            like(cur_query),
            like(cur_key),
            like(cur_value),
            like(half_key),
            like(half_value),
            like(quart_key),
            like(quart_value),
            like(section_bias),
        ),
        in_specs=[vmem] * 3,
        out_specs=(vmem,) * 8,
        compiler_params=pltpu.CompilerParams(vmem_limit_bytes=62 << 20),
        name="finish",
    )(dq, dkv, bias)


def solution(mesh):
    n_z = 4
    n_x = mesh.shape["seq"] // (2 * CHIPS * n_z)
    return jax.shard_map(
        functools.partial(shards, n_x=n_x, n_z=n_z),
        mesh=mesh,
        in_specs=(
            P("seq", "head"),
            P("seq", "head"),
            P("seq", "head"),
            P("seq", "head"),
            P(None, "head"),
            P("seq", "head"),
            P("seq", "head"),
            P("seq", "head"),
            P("seq", "head"),
            P(),
            P(None, "head"),
        ),
        out_specs=(
            P("seq", "head"),
            P("seq", "head"),
            P("seq", "head"),
            P("seq", "head"),
            P("seq", "head"),
            P("seq", "head"),
            P("seq", "head"),
            P(None, "head"),
        ),
        check_vma=False,
    )
```

```python
import functools

import jax
import jax.numpy as jnp
from jax import lax
from jax.experimental import pallas as pl
from jax.experimental.pallas import tpu as pltpu
from jax.sharding import PartitionSpec as P

HD = 64
LANES = 128
CHIPS = 4
HEADS = 3
FAR = 3
MESH = pl.DeviceIdType.MESH
BF = jnp.bfloat16
F32 = jnp.float32


def dot(a, b, ca, cb):
    return lax.dot_general(a, b, (((ca,), (cb,)), ((), ())), preferred_element_type=F32)


def joined(a, head_a, b, head_b):
    return jnp.concatenate(
        [a[:, head_a * HD : (head_a + 1) * HD], b[:, head_b * HD : (head_b + 1) * HD]], axis=1
    )


def exchange_kernel(
    n_x,
    n_z,
    query_hbm,
    key_hbm,
    value_hbm,
    grad_hbm,
    weight_hbm,
    half_key_hbm,
    half_value_hbm,
    quart_key_hbm,
    quart_value_hbm,
    counts_hbm,
    section_bias_hbm,
    dq_out,
    dkv_out,
    bias_out,
    query,
    key,
    value,
    grad,
    grad_far,
    weight,
    half_key,
    half_value,
    quart_key,
    quart_value,
    counts,
    section_bias,
    kv_send,
    qa_send,
    kv_all,
    qa_all,
    count_bias,
    tops,
    scores,
    d_probs,
    low,
    part_send,
    part_got,
    own_sum,
    dkv_send,
    dq_send,
    bias_send,
    bias_zc,
    bias_xy,
    load_sem,
    z_ss,
    z_rs,
    kv_ss,
    kv_rs,
    sib_ss,
    sib_rs,
    fwd_ss,
    fwd_rs,
    qa_ss,
    qa_rs,
    part_ss,
    part_rs,
    dkv_ss,
    dkv_rs,
    dq_ss,
    dq_rs,
    zc_ss,
    zc_rs,
    xy_ss,
    xy_rs,
    round_sem,
):
    rows = query_hbm.shape[0]
    half_rows = half_key_hbm.shape[0]
    quart_rows = quart_key_hbm.shape[0]
    width = query_hbm.shape[1]
    block = kv_send.shape[1]
    quart_at = block - 16
    heads = width // HD
    seq = lax.axis_index("seq")
    head = lax.axis_index("head")
    core = seq % 2
    y = seq // 2 % CHIPS
    z = seq // 8 % n_z
    x = seq // (8 * n_z)
    clip = seq // 8

    def device(x, z, y, core):
        return ((x * n_z + z) * CHIPS + y) * 2 + core

    def chip(dy):
        return (y + dy) % CHIPS

    def copy(src, dst, ss, rs, seq_to, head_to=None):
        return pltpu.make_async_remote_copy(
            src_ref=src,
            dst_ref=dst,
            send_sem=ss,
            recv_sem=rs,
            device_id={"seq": seq_to, "head": head if head_to is None else head_to},
            device_id_type=MESH,
        )

    loads = [
        pltpu.make_async_copy(a, b, load_sem.at[i])
        for i, (a, b) in enumerate(
            [
                (query_hbm, query),
                (key_hbm, key),
                (value_hbm, value),
                (half_key_hbm, half_key),
                (half_value_hbm, half_value),
                (quart_key_hbm, quart_key),
                (quart_value_hbm, quart_value),
                (counts_hbm, counts),
                (section_bias_hbm, section_bias),
                (grad_hbm, grad),
                (weight_hbm, weight),
            ]
        )
    ]
    for load in loads:
        load.start()

    sibling = device(x, z, y, 1 - core)
    zc_peers = [
        device(x, (z + d) % n_z, y, (core + p) % 2) for d in range(n_z) for p in range(2)
    ][1:]
    xy_peers = [device((x + d) % n_x, z, chip(dy), core) for d in range(n_x) for dy in range(CHIPS)][1:]
    near_peers = [sibling] + [device(x, z, chip(dy), core) for dy in range(1, CHIPS)]
    near_peers += [device((x + d) % n_x, z, y, core) for d in (1, n_x - 1)]
    near_peers += [device(x, (z + d) % n_z, y, core) for d in (1, n_z - 1)]
    partners = [(seq, 1 - head)] + [(peer, head) for peer in near_peers]
    barrier = pltpu.get_barrier_semaphore()
    for seq_to, head_to in partners:
        pl.semaphore_signal(
            barrier, inc=1, device_id={"seq": seq_to, "head": head_to}, device_id_type=MESH
        )

    for load in loads[:7]:
        load.wait()
    zeros = jnp.zeros((block - rows, LANES), BF)
    for h in range(heads):
        first, second = (value, key) if h % HEADS == 1 else (key, value)
        kv_send[h, :rows] = joined(first, h, second, h)
        kv_send[h, rows:] = zeros
        first, second = (half_value, half_key) if h % HEADS == 1 else (half_key, half_value)
        kv_send[h, rows : rows + half_rows] = joined(first, h, second, h)
        first, second = (quart_value, quart_key) if h % HEADS == 1 else (quart_key, quart_value)
        kv_send[h, quart_at : quart_at + quart_rows] = joined(first, h, second, h)
    query[...] = query[...] * BF(HD**-0.5)
    for c in range(CHIPS):
        qa_send[HEADS * c] = joined(query, HEADS * c, query, HEADS * c + 1)

    pl.semaphore_wait(barrier, len(partners))

    far_cols = width // FAR
    z_copies = []
    for i in range(FAR):
        cols = slice(i * far_cols, (i + 1) * far_cols)
        c = copy(
            grad_hbm.at[:, cols], grad_far.at[:, cols], z_ss.at[i], z_rs.at[i], seq, 1 - head
        )
        c.start()
        z_copies.append(c)
    qa_copies = {}

    def greet(i):
        for peer in near_peers:
            pl.semaphore_signal(
                round_sem.at[i], inc=1, device_id={"seq": peer, "head": head}, device_id_type=MESH
            )

    def greeted(i):
        pl.semaphore_wait(round_sem.at[i], len(near_peers))

    def send_tile(t):
        for dy in (2, 1, 3):
            c = copy(
                qa_send.at[HEADS * chip(dy) + t],
                qa_all.at[t, dy],
                qa_ss.at[t, dy],
                qa_rs.at[t, dy],
                device(x, z, chip(dy), core),
            )
            c.start()
            qa_copies[t, dy] = c
        qa_all[t, 0] = qa_send[HEADS * y + t]

    send_tile(0)
    kv_copies = {}
    sib_copies = []
    for j in range(HEADS):
        for dy in (2, 1, 3):
            c = copy(
                kv_send.at[HEADS * chip(dy) + j],
                kv_all.at[j, 0, dy],
                kv_ss.at[j, dy],
                kv_rs.at[j, dy],
                device(x, z, chip(dy), core),
            )
            c.start()
            kv_copies[j, dy] = c
        c = copy(
            kv_send.at[HEADS * y + j], kv_all.at[j, 1, 0], sib_ss.at[j], sib_rs.at[j], sibling
        )
        c.start()
        sib_copies.append(c)
        kv_all[j, 0, 0] = kv_send[HEADS * y + j]

    greet(0)
    loads[7].wait()
    loads[8].wait()
    row_id = lax.broadcasted_iota(jnp.int32, (rows, LANES), 0)
    for c in range(2 * CHIPS):
        p, dy = divmod(c, CHIPS)
        shard = 2 * chip(CHIPS - dy) + (core if p == 0 else 1 - core)
        count_bias[c] = jnp.where(row_id < counts[shard, clip], F32(0), F32(-1e30))

    loads[9].wait()
    loads[10].wait()
    adjoint = dot(grad[...], weight[pl.ds(pl.multiple_of(head * width, LANES), width), :], 1, 0)

    fwd_copies = {}

    def forward(j):
        for dy in (2, 1, 3):
            kv_copies[j, dy].wait_recv()
            c = copy(
                kv_all.at[j, 0, dy],
                kv_all.at[j, 1, dy],
                fwd_ss.at[j, dy],
                fwd_rs.at[j, dy],
                sibling,
            )
            c.start()
            fwd_copies[j, dy] = c

    forward(0)
    for i in range(FAR):
        z_copies[i].wait_recv()
        at = pl.multiple_of((1 - head) * width + i * far_cols, LANES)
        adjoint += dot(
            grad_far[:, i * far_cols : (i + 1) * far_cols], weight[pl.ds(at, far_cols), :], 1, 0
        )
    own_count = counts[2 * y + core, clip]
    row_wide = lax.broadcasted_iota(jnp.int32, (rows, width), 0)
    adjoint = jnp.where(row_wide < own_count, adjoint, F32(0)).astype(BF)
    for c in range(CHIPS):
        qa_send[HEADS * c + 1] = joined(adjoint, HEADS * c + 1, adjoint, HEADS * c)
    send_tile(1)
    for c in range(CHIPS):
        qa_send[HEADS * c + 2] = joined(query, HEADS * c + 2, adjoint, HEADS * c + 2)
    send_tile(2)

    bias_row = lax.broadcasted_iota(jnp.int32, (8, LANES), 0)
    bias_lane = lax.broadcasted_iota(jnp.int32, (8, LANES), 1)
    hist_id = lax.broadcasted_iota(jnp.int32, (block - rows, LANES), 0)
    queries = CHIPS * rows
    groups = queries // LANES
    low_lane = lax.broadcasted_iota(jnp.int32, (queries, LANES), 1) < HD

    def fold(t, op):
        total = t[:8]
        for r in range(8, t.shape[0], 8):
            total = op(total, t[r : r + 8])
        return total

    def wait_tile(t):
        for dy in (2, 1, 3):
            qa_copies[t, dy].wait_recv()

    def wait_keys(j):
        for dy in (2, 1, 3):
            fwd_copies[j, dy].wait_recv()
        sib_copies[j].wait_recv()

    def query_part(j):
        tile = qa_all[2 if j == 2 else 0].reshape(queries, LANES)
        return jnp.where(low_lane, BF(0), tile) if j == 1 else jnp.where(low_lane, tile, BF(0))

    def adjoint_part(j):
        tile = qa_all[2 if j == 2 else 1].reshape(queries, LANES)
        return jnp.where(low_lane, tile, BF(0)) if j == 1 else jnp.where(low_lane, BF(0), tile)

    def score_pass(j):
        my_head = HEADS * y + j
        half_bias = section_bias[0, my_head]
        quart_bias = section_bias[1, my_head]
        hist_bias = jnp.where(
            hist_id < half_rows,
            half_bias,
            jnp.where(
                (hist_id >= quart_at - rows) & (hist_id < quart_at - rows + quart_rows),
                quart_bias,
                F32(-1e30),
            ),
        )
        q_part = query_part(j)
        top = jnp.full((8, queries), -3e38, F32)
        for c in range(2 * CHIPS):
            s = dot(kv_all[j, c // CHIPS, c % CHIPS], q_part, 1, 1)
            bias = jnp.concatenate([count_bias[c], hist_bias], axis=0)
            s = s + jnp.concatenate([bias] * groups, axis=1)
            scores[j, c] = s
            top = jnp.maximum(top, fold(s, jnp.maximum))
        tops[j] = top

    def dscore_pass(j):
        a_part = adjoint_part(j)
        top = jnp.max(tops[j], axis=0, keepdims=True)
        total = jnp.zeros((8, queries), F32)
        delta = jnp.zeros((8, queries), F32)
        for c in range(2 * CHIPS):
            dp = dot(kv_all[j, c // CHIPS, c % CHIPS], a_part, 1, 1)
            e = jnp.exp(scores[j, c] - top)
            scores[j, c] = e
            d_probs[c] = dp
            total = total + fold(e, jnp.add)
            delta = delta + fold(e * dp, jnp.add)
        inverse = 1.0 / jnp.sum(total, axis=0, keepdims=True)
        delta = jnp.sum(delta, axis=0, keepdims=True) * inverse
        half_sum = jnp.zeros((8, queries), F32)
        quart_sum = jnp.zeros((8, queries), F32)
        for c in range(2 * CHIPS):
            probs = scores[j, c] * inverse
            ds = probs * (d_probs[c] - delta)
            half_sum = half_sum + fold(ds[rows:quart_at], jnp.add)
            quart_sum = quart_sum + fold(ds[quart_at:], jnp.add)
            low[j, c * block : (c + 1) * block, :queries] = ds.astype(BF)
            low[j, c * block : (c + 1) * block, queries:] = probs.astype(BF)
        return jnp.where(
            bias_lane == HEADS * y + j,
            jnp.where(bias_row == 0, jnp.sum(half_sum), jnp.sum(quart_sum)),
            F32(0),
        )

    part_copies = {}
    out_copies = []
    own_copies = []

    def products(j):
        my_head = HEADS * y + j
        near = CHIPS * block
        both = jnp.concatenate([query_part(j), adjoint_part(j)], axis=0)
        kv = kv_all[j].reshape(2 * near, LANES)
        at = HD if j == 1 else 0
        dq = (dot(kv, low[j, :, :queries], 0, 0)[at : at + HD] * F32(HD**-0.5)).astype(BF)
        for dy in range(CHIPS):
            dq_send[j, dy] = dq[:, dy * rows : (dy + 1) * rows]
        for dy in (2, 1, 3):
            c = copy(
                dq_send.at[j, dy],
                dq_out.at[my_head],
                dq_ss.at[j, dy],
                dq_rs.at[j, dy],
                device(x, z, chip(CHIPS - dy), core),
            )
            c.start()
            out_copies.append(c)
        c = pltpu.make_async_copy(dq_send.at[j, 0], dq_out.at[my_head], dq_ss.at[j, 0])
        c.start()
        own_copies.append(c)
        grads = dot(both, low[j], 0, 1).T
        part_send[j] = grads[near:].astype(BF)
        c = copy(part_send.at[j], part_got.at[j], part_ss.at[j], part_rs.at[j], sibling)
        c.start()
        part_copies[j] = c
        own_sum[j] = grads[:near]

    def send_keys(j):
        my_head = HEADS * y + j
        part_copies[j].wait()
        for dy in (2, 1, 3, 0):
            at = slice(dy * block, (dy + 1) * block)
            dkv_send[j, dy] = (own_sum[j, at] + part_got[j, at].astype(F32)).astype(BF)
            if dy == 0:
                c = pltpu.make_async_copy(dkv_send.at[j, 0], dkv_out.at[my_head], dkv_ss.at[j, 0])
                c.start()
                own_copies.append(c)
                continue
            c = copy(
                dkv_send.at[j, dy],
                dkv_out.at[my_head],
                dkv_ss.at[j, dy],
                dkv_rs.at[j, dy],
                device(x, z, chip(CHIPS - dy), core),
            )
            c.start()
            out_copies.append(c)

    def spread(total, stage, peers, slots, me, ss, rs):
        bias_send[stage] = total
        slots[me] = total
        copies = []
        for i, peer in enumerate(peers):
            c = copy(bias_send.at[stage], slots.at[me], ss.at[i], rs.at[i], peer)
            c.start()
            copies.append(c)
        return copies

    def gathered(slots, copies):
        for c in copies:
            c.wait()
        total = slots[0]
        for i in range(1, len(copies) + 1):
            total = total + slots[i]
        return total

    greeted(0)
    greet(1)
    wait_tile(0)
    wait_keys(0)
    score_pass(0)
    forward(1)
    wait_keys(1)
    score_pass(1)
    forward(2)
    wait_tile(1)
    bias_total = dscore_pass(0)
    products(0)
    bias_total = bias_total + dscore_pass(1)
    send_keys(0)
    wait_keys(2)
    wait_tile(2)
    score_pass(2)
    bias_total = bias_total + dscore_pass(2)
    greeted(1)
    zc_copies = spread(bias_total, 0, zc_peers, bias_zc, 2 * z + core, zc_ss, zc_rs)
    products(1)
    products(2)
    send_keys(1)
    send_keys(2)
    bias_total = gathered(bias_zc, zc_copies)
    xy_copies = spread(bias_total, 1, xy_peers, bias_xy, CHIPS * x + y, xy_ss, xy_rs)
    bias_out[...] = gathered(bias_xy, xy_copies)

    for c in kv_copies.values():
        c.wait_send()
    for c in sib_copies:
        c.wait_send()
    for c in fwd_copies.values():
        c.wait_send()
    for c in qa_copies.values():
        c.wait_send()
    for c in z_copies:
        c.wait_send()
    for c in own_copies + out_copies:
        c.wait()


def finish_kernel(
    half_rows,
    quart_rows,
    dq,
    dkv,
    bias,
    d_query,
    d_key,
    d_value,
    d_half_key,
    d_half_value,
    d_quart_key,
    d_quart_value,
    d_bias,
):
    heads = dq.shape[0]
    rows = d_key.shape[0]
    quart_at = dkv.shape[1] - 16
    for i in range(heads // 2):
        cols = slice(i * LANES, (i + 1) * LANES)
        d_query[:, cols] = dq[2 * i : 2 * i + 2].reshape(LANES, rows).T
        low, high = dkv[2 * i], dkv[2 * i + 1]
        swap_low, swap_high = 2 * i % HEADS == 1, (2 * i + 1) % HEADS == 1
        for value, outs in (
            (0, (d_key, d_half_key, d_quart_key)),
            (1, (d_value, d_half_value, d_quart_value)),
        ):
            both = joined(low, value ^ swap_low, high, value ^ swap_high)
            outs[0][:, cols] = both[:rows]
            outs[1][:, cols] = both[rows : rows + half_rows]
            outs[2][:, cols] = both[quart_at : quart_at + quart_rows]
    d_bias[...] = bias[: d_bias.shape[0], : d_bias.shape[1]]


def shards(
    cur_query,
    cur_key,
    cur_value,
    grad_out,
    out_weight,
    half_key,
    half_value,
    quart_key,
    quart_value,
    cur_count,
    section_bias,
    n_x,
    n_z,
):
    rows, width = cur_query.shape
    half_rows, quart_rows = half_key.shape[0], quart_key.shape[0]
    heads = width // HD
    block = rows + 48
    counts = cur_count.T
    hbm = pl.BlockSpec(memory_space=pltpu.HBM)
    vmem = pl.BlockSpec(memory_space=pltpu.VMEM)
    dma = pltpu.SemaphoreType.DMA
    queries = CHIPS * rows
    shards_n = 2 * CHIPS
    pair = [dma((HEADS, CHIPS)), dma((HEADS, CHIPS))]
    triple = [dma((HEADS,)), dma((HEADS,))]
    dq, dkv, bias = pl.pallas_call(
        functools.partial(exchange_kernel, n_x, n_z),
        out_shape=(
            jax.ShapeDtypeStruct((heads, HD, rows), BF),
            jax.ShapeDtypeStruct((heads, block, LANES), BF),
            jax.ShapeDtypeStruct((8, LANES), F32),
        ),
        in_specs=[hbm] * 11,
        out_specs=(hbm, hbm, vmem),
        scratch_shapes=[
            pltpu.VMEM((rows, width), BF),
            pltpu.VMEM((rows, width), BF),
            pltpu.VMEM((rows, width), BF),
            pltpu.VMEM((rows, width), BF),
            pltpu.VMEM((rows, width), BF),
            pltpu.VMEM(out_weight.shape, BF),
            pltpu.VMEM(half_key.shape, BF),
            pltpu.VMEM(half_value.shape, BF),
            pltpu.VMEM(quart_key.shape, BF),
            pltpu.VMEM(quart_value.shape, BF),
            pltpu.SMEM(counts.shape, jnp.int32),
            pltpu.SMEM(section_bias.shape, F32),
            pltpu.VMEM((heads, block, LANES), BF),
            pltpu.VMEM((heads, rows, LANES), BF),
            pltpu.VMEM((HEADS, 2, CHIPS, block, LANES), BF),
            pltpu.VMEM((HEADS, CHIPS, rows, LANES), BF),
            pltpu.VMEM((shards_n, rows, LANES), F32),
            pltpu.VMEM((HEADS, 8, queries), F32),
            pltpu.VMEM((HEADS, shards_n, block, queries), F32),
            pltpu.VMEM((shards_n, block, queries), F32),
            pltpu.VMEM((HEADS, shards_n * block, 2 * queries), BF),
            pltpu.VMEM((HEADS, CHIPS * block, LANES), BF),
            pltpu.VMEM((HEADS, CHIPS * block, LANES), BF),
            pltpu.VMEM((HEADS, CHIPS * block, LANES), F32),
            pltpu.VMEM((HEADS, CHIPS, block, LANES), BF),
            pltpu.VMEM((HEADS, CHIPS, HD, rows), BF),
            pltpu.VMEM((2, 8, LANES), F32),
            pltpu.VMEM((2 * n_z, 8, LANES), F32),
            pltpu.VMEM((n_x * CHIPS, 8, LANES), F32),
            dma((11,)),
            dma((FAR,)),
            dma((FAR,)),
            *pair,
            *triple,
            *pair,
            *pair,
            *triple,
            *pair,
            *pair,
            dma((2 * n_z,)),
            dma((2 * n_z,)),
            dma((n_x * CHIPS,)),
            dma((n_x * CHIPS,)),
            pltpu.SemaphoreType.REGULAR((2,)),
        ],
        compiler_params=pltpu.CompilerParams(
            collective_id=0, has_side_effects=True, vmem_limit_bytes=62 << 20
        ),
        name="exchange",
    )(
        cur_query,
        cur_key,
        cur_value,
        grad_out,
        out_weight,
        half_key,
        half_value,
        quart_key,
        quart_value,
        counts,
        section_bias,
    )
    like = lambda a: jax.ShapeDtypeStruct(a.shape, a.dtype)
    return pl.pallas_call(
        functools.partial(finish_kernel, half_rows, quart_rows),
        out_shape=(
            like(cur_query),
            like(cur_key),
            like(cur_value),
            like(half_key),
            like(half_value),
            like(quart_key),
            like(quart_value),
            like(section_bias),
        ),
        grid=(2,),
        in_specs=[
            pl.BlockSpec((heads // 2, HD, rows), lambda i: (i, 0, 0)),
            pl.BlockSpec((heads // 2, block, LANES), lambda i: (i, 0, 0)),
            pl.BlockSpec((8, LANES), lambda i: (0, 0)),
        ],
        out_specs=(
            *[pl.BlockSpec((n, width // 2), lambda i: (0, i)) for n in [rows] * 3],
            *[pl.BlockSpec((half_rows, width // 2), lambda i: (0, i))] * 2,
            *[pl.BlockSpec((quart_rows, width // 2), lambda i: (0, i))] * 2,
            pl.BlockSpec(section_bias.shape, lambda i: (0, 0)),
        ),
        compiler_params=pltpu.CompilerParams(vmem_limit_bytes=62 << 20),
        name="finish",
    )(dq, dkv, bias)


def solution(mesh):
    n_z = 4
    n_x = mesh.shape["seq"] // (2 * CHIPS * n_z)
    return jax.shard_map(
        functools.partial(shards, n_x=n_x, n_z=n_z),
        mesh=mesh,
        in_specs=(
            P("seq", "head"),
            P("seq", "head"),
            P("seq", "head"),
            P("seq", "head"),
            P(None, "head"),
            P("seq", "head"),
            P("seq", "head"),
            P("seq", "head"),
            P("seq", "head"),
            P(),
            P(None, "head"),
        ),
        out_specs=(
            P("seq", "head"),
            P("seq", "head"),
            P("seq", "head"),
            P("seq", "head"),
            P("seq", "head"),
            P("seq", "head"),
            P("seq", "head"),
            P(None, "head"),
        ),
        check_vma=False,
    )
```
